256 devices in a mesh: stn: 64 (over z, y_hi, x), chan: 4 (over y_lo, core).
Axes of the slice: x: 4, y: 4 (y_hi: 2, y_lo: 2; y = y_hi * 2 + y_lo), z: 8, core: 2. Of those that a mesh axis runs over, the one named last changes fastest.
Arguments:
- samples: bfloat16 [512, 17, 2, 8192], P(('stn', 'chan')), may hold values from -6 to 6
- keeper: int32 [64, 64], replicated, may hold values from 0 to 1, as said below
Outputs:
- visibilities: bfloat16 [512, 2, 4096, 264], P('stn', None, 'chan')
The draws below stay inside these ranges and needn't reach their ends.
Inputs may be any that keep to these rules, and one draw needn't show every extreme that they name: keeper[g, g] is 1; for g != h with d = (g - h) mod 64: keeper[g, h] is 1 where 0 < d < 32, 0 where d > 32, and at d = 32 exactly one of keeper[g, h] and keeper[h, g] is 1, which one drawn for each such pair; half of the rows hold 33 ones, the others 33 - 1.
All inputs are finite; a program needn't handle non-finite values.
Results may differ from the reference program's by a relative error of at most 0.0077.
Values may be sent and summed in bfloat16 or wider, within the bound.
No kernel may reach another device: no remote copies, remote signals or barrier semaphores. Data moves between devices by JAX's collectives and lax.ppermute only.
A program may use at most 192 MiB of HBM per device.

```python
import math
import jax
import jax.numpy as jnp
from jax import lax

NFFT = 8192
TAPS = 16
STN_DEV = 1
CH_WIN = 1024
DFT_BLOCK = 256
FRAMES = 2
FRAMES_IN = 17
GROUPS = 64
INPUTS = 512
N_STN = 64
N_CHAN = 4


def draw_keeper(key, part):
    middle = GROUPS // 2
    coins = jax.random.randint(jax.random.fold_in(key, 11), (middle,), 0, 2).astype(jnp.int32)
    first = jnp.arange(GROUPS, dtype=jnp.int32)[:, None]
    second = jnp.arange(GROUPS, dtype=jnp.int32)[None, :]
    distance = (first - second) % GROUPS
    coin_row = jnp.take(coins, first % middle)
    lower_wins = (first < second) == (coin_row == 0)
    kept = (distance == 0) | (distance >= 1) & (distance < middle) | (distance == middle) & lower_wins
    return kept.astype(jnp.int32)


def block_levels(rng, dims, pieces, low, largest):
    def one(axis_at, blocks):
        heights = jax.random.uniform(jax.random.fold_in(jax.random.fold_in(rng, 6), axis_at), (blocks,), jnp.float32, low / len(pieces), largest / len(pieces))
        return jnp.repeat(jnp.exp(heights), dims[axis_at] // blocks).reshape((-1,) + (1,) * (len(dims) - axis_at - 1))

    loudness = one(*pieces[0])
    for cut in pieces[1:]:
        loudness = loudness * one(*cut)
    return loudness


def bell_draw(stream_key, dims, scale, limit, split=(), kind=jnp.bfloat16):
    factor_of = block_levels(stream_key, dims, split, -0.22, 0.18) if split else 1.0
    entries = jax.random.normal(stream_key, dims, jnp.float32) * scale * factor_of
    return jnp.minimum(jnp.maximum(entries, -limit), limit).astype(kind)


def setup_inputs(seed: int = 0) -> dict:
    key_list = jax.random.split(jax.random.key(seed), 3)
    return {
        "samples": bell_draw(key_list[0], (INPUTS, FRAMES_IN, 2, NFFT), 1.0, 6.0, ((0, 256),)),
        "keeper": draw_keeper(jax.random.fold_in(key_list[2], 71), 0),
    }


def taps_table():
    pos = jnp.arange(TAPS * NFFT).astype(jnp.float32)
    shifted = (pos + 0.5) / NFFT - TAPS / 2.0
    window = 0.5 - 0.5 * jnp.cos(2.0 * math.pi * (pos + 0.5) / (TAPS * NFFT))
    return (jnp.sinc(shifted) * window).reshape(TAPS, NFFT)

def twiddles(width):
    index_n = jnp.arange(NFFT, dtype=jnp.int32)[:, None]
    index_k = jnp.arange(width, dtype=jnp.int32)[None, :]
    phase = (index_n * index_k % NFFT).astype(jnp.float32) * (2.0 * math.pi / NFFT)
    cosines = jnp.cos(phase).astype(jnp.bfloat16)
    sines = jnp.sin(phase).astype(jnp.bfloat16)
    upper = jnp.concatenate([cosines, -sines], axis=1)
    lower = jnp.concatenate([sines, cosines], axis=1)
    return jnp.concatenate([upper, lower], axis=0)

def rotations(ch_tot, width):
    blocks = ch_tot // width
    index_n = jnp.arange(NFFT, dtype=jnp.int32)[None, :]
    index_b = jnp.arange(blocks, dtype=jnp.int32)[:, None]
    phase = (index_n * index_b * width % NFFT).astype(jnp.float32) * (2.0 * math.pi / NFFT)
    return (jnp.cos(phase), jnp.sin(phase))

def channelise(block, taps, table, cos_rot, sin_rot, ch_tot):
    frames = block.shape[1] - TAPS + 1
    count = block.shape[0]
    width = table.shape[1] // 2
    blocks = ch_tot // width
    total = taps[0] * block[:, 0:frames].astype(jnp.float32)
    for tap in range(1, TAPS):
        total = total + taps[tap] * block[:, tap:tap + frames].astype(jnp.float32)
    real_part = total[:, :, 0][None]
    imag_part = total[:, :, 1][None]
    cosine = cos_rot[:, None, None, :]
    sine = sin_rot[:, None, None, :]
    rot_real = real_part * cosine + imag_part * sine
    rot_imag = imag_part * cosine - real_part * sine
    lhs = jnp.stack([rot_real, rot_imag], axis=3).astype(jnp.bfloat16)
    lhs = lhs.reshape(blocks * count * frames, 2 * NFFT)
    spectrum = jnp.dot(lhs, table, preferred_element_type=jnp.float32) * (1.0 / math.sqrt(NFFT))
    spectrum = spectrum.astype(jnp.bfloat16).reshape(blocks, count, frames, 2, width)
    spectrum = jnp.transpose(spectrum, (1, 0, 4, 3, 2))
    return spectrum.reshape(count, ch_tot, 2, frames)

def correlate(own, others, frames):
    half = others.shape[2] // 2
    turned = jnp.concatenate([-others[:, :, half:], others[:, :, :half]], axis=2)
    rhs = jnp.concatenate([others, turned], axis=0)
    product = lax.dot_general(own.astype(jnp.float32), rhs.astype(jnp.float32), (((2,), (2,)), ((1,), (1,))))
    rows = others.shape[0]
    product = product.reshape(product.shape[0], product.shape[1], 2, rows)
    return jnp.transpose(product, (1, 2, 0, 3)) / frames

def slot_table(keep_rows, keep_slots):
    ranking = (jnp.cumsum(keep_rows, axis=1) - 1).astype(jnp.int32)
    slot_index = jnp.arange(keep_slots, dtype=jnp.int32)
    matched = (keep_rows[:, :, None] == 1) & (ranking[:, :, None] == slot_index[None, None, :])
    column_ids = jnp.arange(keep_rows.shape[1], dtype=jnp.int32)
    slot_column = lax.optimization_barrier(jnp.sum(jnp.where(matched, column_ids[None, :, None], 0), axis=1)).astype(jnp.int32)
    filled = jnp.any(matched, axis=1)
    return (slot_column, filled)

def reference(samples, keeper):
    ch_tot = CH_WIN * N_CHAN
    inputs = samples.shape[0]
    group_in = 2 * STN_DEV * N_CHAN
    keep_slots = N_STN // 2 + 1
    taps = taps_table()
    table = twiddles(DFT_BLOCK)
    cos_rot, sin_rot = rotations(ch_tot, DFT_BLOCK)
    per_block = 2 * STN_DEV
    blocks = samples.reshape(inputs // per_block, per_block, FRAMES_IN, 2, NFFT)
    spectra = lax.map(lambda block: channelise(block, taps, table, cos_rot, sin_rot, ch_tot), blocks)
    spectra = spectra.reshape(inputs, ch_tot, 2 * FRAMES)
    slot_column, filled = slot_table(keeper, keep_slots)
    span_ch = 16

    def one_step(step, result):
        start = (step * span_ch).astype(jnp.int32)
        part = lax.dynamic_slice_in_dim(spectra, start, span_ch, 1)
        tile = correlate(part, part, FRAMES)
        tile = tile.reshape(N_STN, group_in, 2, span_ch, N_STN, group_in)
        picked = jnp.take_along_axis(tile, slot_column[:, None, None, None, :, None], axis=4)
        picked = jnp.where(filled[:, None, None, None, :, None], picked, jnp.zeros((), jnp.float32))
        picked = picked.reshape(inputs, 2, span_ch, keep_slots * group_in).astype(jnp.bfloat16)
        return lax.dynamic_update_slice_in_dim(result, picked, start, 2)
    result = jnp.zeros((inputs, 2, ch_tot, keep_slots * group_in), jnp.bfloat16)
    return lax.fori_loop(0, ch_tot // span_ch, one_step, result)
```

```python
import functools
import math

import jax
import jax.numpy as jnp
import numpy as np
from jax import lax
from jax.experimental import pallas as pl
from jax.experimental.pallas import tpu as pltpu
from jax.sharding import PartitionSpec as P

NFFT = 8192
TAPS = 16
CH_WIN = 1024
N_Z, N_Y, N_X = 8, 2, 4
MIB = 1 << 20
SMEM = pltpu.MemorySpace.SMEM
VMEM = pltpu.MemorySpace.VMEM


def filter_taps():
    pos = np.arange(TAPS * NFFT, dtype=np.float64)
    shifted = (pos + 0.5) / NFFT - TAPS / 2.0
    window = 0.5 - 0.5 * np.cos(2.0 * math.pi * (pos + 0.5) / (TAPS * NFFT))
    taps = (np.sinc(shifted) * window).reshape(TAPS, 64, 1, 128)
    return np.broadcast_to(taps, (TAPS, 64, 2, 128)).reshape(TAPS, 128, 128).astype(np.float32)


def transform_tables():
    k1 = np.arange(64)
    angle = 2.0 * math.pi * (np.outer(k1, k1) % 64) / 64
    cos, sin = np.cos(angle), np.sin(angle)
    first = np.zeros((2, 64, 64, 2))
    first[0, :, :, 0], first[0, :, :, 1] = cos, sin
    first[1, :, :, 0], first[1, :, :, 1] = -sin, cos
    n2 = np.arange(128)
    turn = 2.0 * math.pi * np.outer(k1, n2) / NFFT
    k2 = np.arange(64)
    angle = 2.0 * math.pi * (np.outer(k2, n2) % 128) / 128
    cos = (np.cos(angle) / math.sqrt(NFFT)).reshape(32, 2, 128).transpose(1, 0, 2)
    sin = (np.sin(angle) / math.sqrt(NFFT)).reshape(32, 2, 128).transpose(1, 0, 2)
    second = np.zeros((2, 2, 32, 2, 128))
    second[:, 0, :, 0], second[:, 0, :, 1] = cos, sin
    second[:, 1, :, 0], second[:, 1, :, 1] = -sin, cos
    return (
        first.reshape(128, 128).astype(np.float32),
        np.stack([np.cos(turn), np.sin(turn)]).astype(np.float32),
        second.reshape(128, 256).astype(np.float32),
    )


def spectra_kernel(x_ref, taps_ref, first_ref, turn_ref, second_ref, out_ref, rows_ref):
    turned = []
    for i in range(2):
        for f in range(2):
            total = taps_ref[0] * x_ref[i, f].astype(jnp.float32)
            for tap in range(1, TAPS):
                total = total + taps_ref[tap] * x_ref[i, f + tap].astype(jnp.float32)
            y = jnp.dot(
                first_ref[...], total, precision=lax.Precision.HIGHEST, preferred_element_type=jnp.float32
            )
            re, im = y[:64], y[64:]
            cos, sin = turn_ref[0], turn_ref[1]
            turned.append(jnp.concatenate([re * cos + im * sin, im * cos - re * sin], axis=1))
    z = jnp.concatenate(turned, axis=0)
    o = lax.dot_general(
        second_ref[...], z, (((1,), (1,)), ((), ())),
        precision=lax.Precision.HIGHEST, preferred_element_type=jnp.float32,
    )
    for p in range(2):
        for i in range(2):
            for f in range(2):
                at = (i * 2 + f) * 64
                even = o[p * 32 : p * 32 + 32, at : at + 64]
                odd = o[64 + p * 32 : 64 + p * 32 + 32, at : at + 64]
                s = jnp.concatenate([even, odd], axis=1)
                row = (p * 2 + f) * 2 + i
                for k in range(32):
                    lane = (k % 8) * 128
                    rows_ref[k // 8, row : row + 1, lane : lane + 128] = s[k : k + 1]
    out_ref[...] = rows_ref[...].astype(jnp.bfloat16)


def spectra(samples):
    x = samples.reshape(2, 17, 2, 64, 128).transpose(0, 1, 3, 2, 4).reshape(2, 17, 128, 128)
    first, turn, second = transform_tables()
    return pl.pallas_call(
        spectra_kernel,
        out_shape=jax.ShapeDtypeStruct((4, 8, CH_WIN), jnp.bfloat16),
        in_specs=[pl.BlockSpec(memory_space=VMEM)] * 5,
        out_specs=pl.BlockSpec(memory_space=VMEM),
        scratch_shapes=[pltpu.VMEM((4, 8, CH_WIN), jnp.float32)],
        compiler_params=pltpu.CompilerParams(vmem_limit_bytes=24 * MIB),
        name="spectra",
    )(x, jnp.asarray(filter_taps()), jnp.asarray(first), jnp.asarray(turn), jnp.asarray(second))


def group_kernel(chan_ref, *refs):
    pieces, out_ref, wide_ref, rows_ref = refs[:4], refs[4], refs[5], refs[6]
    for d in range(4):
        wide_ref[d] = pieces[d][...].astype(jnp.float32)
    for source in range(4):
        piece = wide_ref[lax.rem(chan_ref[0] + 4 - source, 4)]
        for t in range(4):
            rows_ref[t, source * 2 : source * 2 + 2, :] = piece[t * 2 : t * 2 + 2]
    out_ref[...] = rows_ref[...].reshape(32, CH_WIN).astype(jnp.bfloat16)


def group_spectra(pieces):
    chan = lax.axis_index("chan").astype(jnp.int32).reshape(1)
    return pl.pallas_call(
        group_kernel,
        out_shape=jax.ShapeDtypeStruct((32, CH_WIN), jnp.bfloat16),
        in_specs=[pl.BlockSpec(memory_space=SMEM)] + [pl.BlockSpec(memory_space=VMEM)] * 4,
        out_specs=pl.BlockSpec(memory_space=VMEM),
        scratch_shapes=[pltpu.VMEM((4, 8, CH_WIN), jnp.float32)] * 2,
        compiler_params=pltpu.CompilerParams(vmem_limit_bytes=8 * MIB),
        name="group_spectra",
    )(chan, *pieces)


def tiles_kernel(base, picks, n_blocks, aliased, *refs):
    slots_ref, own_ref = refs[:2]
    blocks = refs[2 : 2 + n_blocks]
    out_ref, wide_ref, tile_ref, sems = refs[2 + n_blocks + (1 if aliased else 0) :]
    own = own_ref[...].astype(jnp.float32) * 0.5
    for t in range(4):
        for i in range(8):
            wide_ref[i, t] = jnp.broadcast_to(own[t * 8 + i : t * 8 + i + 1], (8, CH_WIN))
    copies = []
    for n, (which, index) in enumerate(picks):
        keep = slots_ref[1, base + n].astype(jnp.float32)

        @pl.loop(0, CH_WIN // 128)
        def _(step):
            lanes = pl.ds(pl.multiple_of(step * 128, 128), 128)
            other = blocks[which][index, :, lanes].astype(jnp.float32) * keep
            r0, r1, i0, i1 = (other[t * 8 : t * 8 + 8] for t in range(4))
            for i in range(8):
                a0, a1, b0, b1 = (wide_ref[i, t, :, lanes] for t in range(4))
                tile_ref[n, i, 0, :, lanes] = ((a0 * r0 + a1 * r1) + (b0 * i0 + b1 * i1)).astype(jnp.bfloat16)
                tile_ref[n, i, 1, :, lanes] = ((b0 * r0 + b1 * r1) - (a0 * i0 + a1 * i1)).astype(jnp.bfloat16)

        copy = pltpu.make_async_copy(tile_ref.at[n], out_ref.at[:, :, slots_ref[0, base + n]], sems.at[n])
        copy.start()
        copies.append(copy)
    for copy in copies:
        copy.wait()


def tiles(slots, base, own, blocks, picks, result, n_slots):
    n = len(picks)
    aliased = result is not None
    operands = [slots, own, *blocks] + ([result] if aliased else [])
    specs = [pl.BlockSpec(memory_space=SMEM)] + [pl.BlockSpec(memory_space=VMEM)] * (1 + len(blocks))
    specs += [pl.BlockSpec(memory_space=pl.ANY)] if aliased else []
    return pl.pallas_call(
        functools.partial(tiles_kernel, base, picks, len(blocks), aliased),
        out_shape=jax.ShapeDtypeStruct((8, 2, n_slots, 8, CH_WIN), jnp.bfloat16),
        in_specs=specs,
        out_specs=pl.BlockSpec(memory_space=pl.ANY),
        input_output_aliases={len(operands) - 1: 0} if aliased else {},
        scratch_shapes=[
            pltpu.VMEM((8, 4, 8, CH_WIN), jnp.float32),
            pltpu.VMEM((n, 8, 2, 8, CH_WIN), jnp.bfloat16),
            pltpu.SemaphoreType.DMA((n,)),
        ],
        compiler_params=pltpu.CompilerParams(vmem_limit_bytes=16 * MIB),
        cost_estimate=pl.CostEstimate(flops=n * 5 * 10**7, bytes_accessed=n * 300_000, transcendentals=0),
        name="tiles",
    )(*operands)


def shift(array, dz, dy, dx):
    def place(z, y, x):
        return ((z % N_Z) * N_Y + y % N_Y) * N_X + x % N_X

    pairs = [
        (place(z, y, x), place(z + dz, y + dy, x + dx)) for z in range(N_Z) for y in range(N_Y) for x in range(N_X)
    ]
    return lax.ppermute(array, "stn", pairs)


def per_device(samples, keeper):
    group = lax.axis_index("stn")
    chan = lax.axis_index("chan")
    z, y, x = group // (N_Y * N_X), group // N_X % N_Y, group % N_X
    n_slots = 33

    parts = spectra(samples)
    pieces = []
    for d in range(4):
        part = lax.dynamic_index_in_dim(parts, (chan + d) % 4, 0, keepdims=False)
        pieces.append(part if d == 0 else lax.ppermute(part, "chan", [(c, (c + d) % 4) for c in range(4)]))
    own = group_spectra(pieces)

    z1, z2, z3, z4 = (shift(own, d, 0, 0) for d in (1, 2, 3, 4))
    y1, y2, y3 = (shift(a, 0, 1, 0) for a in (z1, z2, z3))
    ys = shift(jnp.where(y == 0, own, z4), 0, 1, 0)
    ahead, behind, across = jnp.where(x < 3, own, z4), jnp.where(x > 0, z4, own), jnp.where(x < 2, own, z4)
    b1 = jnp.stack([z1, y1, z2, y2])
    f1, m1 = shift(b1, 0, 0, 1), shift(b1, 0, 0, -1)
    ff1, mm1 = shift(f1[:2], 0, 0, 1), shift(m1[2:], 0, 0, -1)
    f2 = shift(jnp.stack([z3, across, y3, ys, ahead]), 0, 0, 1)
    m2 = shift(jnp.stack([y3, ys, z3, behind]), 0, 0, -1)
    ff2, mm2 = shift(f2[:2], 0, 0, 1), shift(m2[:2], 0, 0, -1)

    def where_from(dz, other, dx):
        ry = 1 - y if other else y
        rx = (x - dx) % N_X
        if dz == "near":
            before = ry * N_X + rx < y * N_X + x
            back = jnp.where(before, 0, 4)
        else:
            back = dz
        return ((z - back) % N_Z) * (N_Y * N_X) + ry * N_X + rx

    local = [own[None], z4[None], ys[None], z1[None], y1[None], z2[None], y2[None], z3[None], y3[None]]
    local_from = [(0, 0, 0), (4, 0, 0), ("near", 1, 0), (1, 0, 0), (1, 1, 0), (2, 0, 0), (2, 1, 0), (3, 0, 0), (3, 1, 0)]
    calls = [
        (local, [(n, 0) for n in range(9)], local_from),
        (
            [f1, m1, ff1, mm1],
            [(w, n) for w in (0, 1) for n in range(4)] + [(2, 0), (2, 1), (3, 0), (3, 1)],
            [(1 + n // 2, n % 2, d) for d in (1, -1) for n in range(4)] + [(1, 0, 2), (1, 1, 2), (2, 0, 2), (2, 1, 2)],
        ),
        (
            [f2, m2, ff2, mm2],
            [(0, 0), (0, 2), (0, 3), (0, 4), (1, 0), (1, 1), (1, 2), (1, 3), (2, 0), (2, 1), (3, 0), (3, 1)],
            [(3, 0, 1), (3, 1, 1), ("near", 1, 1), ("near", 0, 1)]
            + [(3, 1, -1), ("near", 1, -1), (3, 0, -1), ("near", 0, -1)]
            + [(3, 0, 2), ("near", 0, 2), (3, 1, 2), ("near", 1, 2)],
        ),
    ]
    origin = jnp.stack([where_from(*o) for call in calls for o in call[2]]).astype(jnp.int32)
    keep_row = lax.dynamic_index_in_dim(keeper, group, 0, keepdims=False)
    columns = jnp.arange(keeper.shape[1], dtype=jnp.int32)[None, :]
    rank = jnp.sum(jnp.where(columns < origin[:, None], keep_row[None, :], 0), axis=1)
    kept = jnp.sum(jnp.where(columns == origin[:, None], keep_row[None, :], 0), axis=1)
    slots = jnp.stack([jnp.where(kept == 1, rank, n_slots - 1), kept]).astype(jnp.int32)

    result, base = None, 0
    for blocks, picks, _ in calls:
        result = tiles(slots, base, own, blocks, picks, result, n_slots)
        base += len(picks)
    return result.reshape(8, 2, n_slots * 8, CH_WIN).swapaxes(2, 3)


def solution(mesh):
    return jax.shard_map(
        per_device,
        mesh=mesh,
        in_specs=(P(("stn", "chan"), None, None, None), P()),
        out_specs=P("stn", None, "chan", None),
        check_vma=False,
    )
```

```python
import functools
import math

import jax
import jax.numpy as jnp
import numpy as np
from jax import lax
from jax.experimental import pallas as pl
from jax.experimental.pallas import tpu as pltpu
from jax.sharding import PartitionSpec as P

NFFT = 8192
TAPS = 16
CH_WIN = 1024
N_Z, N_Y, N_X = 8, 2, 4
MIB = 1 << 20
UNROLL = 8
SMEM = pltpu.MemorySpace.SMEM
VMEM = pltpu.MemorySpace.VMEM
HBM = pltpu.MemorySpace.HBM


def filter_taps():
    pos = np.arange(TAPS * NFFT, dtype=np.float64)
    shifted = (pos + 0.5) / NFFT - TAPS / 2.0
    window = 0.5 - 0.5 * np.cos(2.0 * math.pi * (pos + 0.5) / (TAPS * NFFT))
    taps = (np.sinc(shifted) * window).reshape(TAPS, 64, 1, 128)
    return np.broadcast_to(taps, (TAPS, 64, 2, 128)).reshape(TAPS, 128, 128).astype(np.float32)


def transform_tables():
    k1 = np.arange(64)
    angle = 2.0 * math.pi * (np.outer(k1, k1) % 64) / 64
    cos, sin = np.cos(angle), np.sin(angle)
    first = np.zeros((2, 64, 64, 2))
    first[0, :, :, 0], first[0, :, :, 1] = cos, sin
    first[1, :, :, 0], first[1, :, :, 1] = -sin, cos
    n2 = np.arange(128)
    turn = 2.0 * math.pi * np.outer(k1, n2) / NFFT
    k2 = np.arange(64)
    angle = 2.0 * math.pi * (np.outer(k2, n2) % 128) / 128
    cos = (np.cos(angle) / math.sqrt(NFFT)).reshape(32, 2, 128).transpose(1, 0, 2)
    sin = (np.sin(angle) / math.sqrt(NFFT)).reshape(32, 2, 128).transpose(1, 0, 2)
    second = np.zeros((2, 2, 32, 2, 128))
    second[:, 0, :, 0], second[:, 0, :, 1] = cos, sin
    second[:, 1, :, 0], second[:, 1, :, 1] = -sin, cos
    return (
        first.reshape(128, 128).astype(np.float32),
        np.stack([np.cos(turn), np.sin(turn)]).astype(np.float32),
        second.reshape(128, 256).astype(np.float32),
    )


def spectra_kernel(*refs):
    chan_ref, outs, held, sems, rows_ref = refs[5], refs[6:10], refs[10:15], refs[15], refs[16]
    copies = [pltpu.make_async_copy(refs[n], held[n], sems.at[n]) for n in range(5)]
    for copy in copies:
        copy.start()
    for copy in copies:
        copy.wait()
    x_ref, taps_ref, first_ref, turn_ref, second_ref = held
    turned = []
    for i in range(2):
        for f in range(2):
            total = taps_ref[0] * x_ref[i, f].astype(jnp.float32)
            for tap in range(1, TAPS):
                total = total + taps_ref[tap] * x_ref[i, f + tap].astype(jnp.float32)
            y = jnp.dot(
                first_ref[...], total, precision=lax.Precision.HIGHEST, preferred_element_type=jnp.float32
            )
            re, im = y[:64], y[64:]
            cos, sin = turn_ref[0], turn_ref[1]
            turned.append(jnp.concatenate([re * cos + im * sin, im * cos - re * sin], axis=1))
    z = jnp.concatenate(turned, axis=0)
    o = lax.dot_general(
        second_ref[...], z, (((1,), (1,)), ((), ())),
        precision=lax.Precision.HIGHEST, preferred_element_type=jnp.float32,
    )
    for p in range(2):
        for i in range(2):
            for f in range(2):
                at = (i * 2 + f) * 64
                even = o[p * 32 : p * 32 + 32, at : at + 64]
                odd = o[64 + p * 32 : 64 + p * 32 + 32, at : at + 64]
                s = jnp.concatenate([even, odd], axis=1)
                row = (p * 2 + f) * 2 + i
                for k in range(32):
                    lane = (k % 8) * 128
                    rows_ref[k // 8, row : row + 1, lane : lane + 128] = s[k : k + 1]
    for d in range(4):
        outs[d][...] = rows_ref[lax.rem(chan_ref[0] + d, 4)].astype(jnp.bfloat16)


def spectra(samples, chan):
    x = samples.reshape(2, 17, 2, 64, 128).transpose(0, 1, 3, 2, 4).reshape(2, 17, 128, 128)
    first, turn, second = transform_tables()
    return pl.pallas_call(
        spectra_kernel,
        out_shape=[jax.ShapeDtypeStruct((8, CH_WIN), jnp.bfloat16)] * 4,
        in_specs=[pl.BlockSpec(memory_space=HBM)] * 5 + [pl.BlockSpec(memory_space=SMEM)],
        out_specs=[pl.BlockSpec(memory_space=VMEM)] * 4,
        scratch_shapes=[
            pltpu.VMEM((2, 17, 128, 128), jnp.bfloat16),
            pltpu.VMEM((TAPS, 128, 128), jnp.float32),
            pltpu.VMEM((128, 128), jnp.float32),
            pltpu.VMEM((2, 64, 128), jnp.float32),
            pltpu.VMEM((128, 256), jnp.float32),
            pltpu.SemaphoreType.DMA((5,)),
            pltpu.VMEM((4, 8, CH_WIN), jnp.float32),
        ],
        compiler_params=pltpu.CompilerParams(vmem_limit_bytes=56 * MIB),
        name="spectra",
    )(x, jnp.asarray(filter_taps()), jnp.asarray(first), jnp.asarray(turn), jnp.asarray(second), chan)


def group_kernel(chan_ref, *refs):
    pieces, out_ref, wide_ref, rows_ref = refs[:4], refs[4], refs[5], refs[6]
    for d in range(4):
        wide_ref[d] = pieces[d][...].astype(jnp.float32)
    for source in range(4):
        piece = wide_ref[lax.rem(chan_ref[0] + 4 - source, 4)]
        for t in range(4):
            rows_ref[t, source * 2 : source * 2 + 2, :] = piece[t * 2 : t * 2 + 2]
    out_ref[...] = rows_ref[...].reshape(32, CH_WIN).astype(jnp.bfloat16)


def group_spectra(pieces, chan):
    return pl.pallas_call(
        group_kernel,
        out_shape=jax.ShapeDtypeStruct((32, CH_WIN), jnp.bfloat16),
        in_specs=[pl.BlockSpec(memory_space=SMEM)] + [pl.BlockSpec(memory_space=VMEM)] * 4,
        out_specs=pl.BlockSpec(memory_space=VMEM),
        scratch_shapes=[pltpu.VMEM((4, 8, CH_WIN), jnp.float32)] * 2,
        compiler_params=pltpu.CompilerParams(vmem_limit_bytes=8 * MIB),
        name="group_spectra",
    )(chan, *pieces)


def tiles_kernel(base, counts, aliased, *refs):
    slots_ref, own_ref = refs[:2]
    blocks = refs[2 : 2 + len(counts)]
    out_ref, wide_ref, tile_ref, sems = refs[2 + len(counts) + (1 if aliased else 0) :]
    own = own_ref[...].astype(jnp.float32) * 0.5
    for t in range(4):
        for i in range(8):
            wide_ref[i, t] = jnp.broadcast_to(own[t * 8 + i : t * 8 + i + 1], (8, CH_WIN))

    def copy_of(n):
        return pltpu.make_async_copy(tile_ref.at[n], out_ref.at[:, :, slots_ref[0, base + n]], sems.at[n])

    first = 0
    for block_ref, count in zip(blocks, counts, strict=True):

        @pl.loop(0, count)
        def _(index, block_ref=block_ref, first=first):
            n = first + index
            keep = slots_ref[1, base + n].astype(jnp.float32)

            @pl.loop(0, CH_WIN // 128, unroll=UNROLL)
            def _(step):
                lanes = pl.ds(pl.multiple_of(step * 128, 128), 128)
                other = block_ref[index, :, lanes].astype(jnp.float32) * keep
                r0, r1, i0, i1 = (other[t * 8 : t * 8 + 8] for t in range(4))
                for i in range(8):
                    a0, a1, b0, b1 = (wide_ref[i, t, :, lanes] for t in range(4))
                    tile_ref[n, i, 0, :, lanes] = ((a0 * r0 + a1 * r1) + (b0 * i0 + b1 * i1)).astype(jnp.bfloat16)
                    tile_ref[n, i, 1, :, lanes] = ((b0 * r0 + b1 * r1) - (a0 * i0 + a1 * i1)).astype(jnp.bfloat16)

            copy_of(n).start()

        first += count

    @pl.loop(0, first)
    def _(n):
        copy_of(n).wait()


def tiles(slots, base, own, blocks, result, n_slots):
    counts = [block.shape[0] for block in blocks]
    n = sum(counts)
    aliased = result is not None
    operands = [slots, own, *blocks] + ([result] if aliased else [])
    specs = [pl.BlockSpec(memory_space=SMEM)] + [pl.BlockSpec(memory_space=VMEM)] * (1 + len(blocks))
    specs += [pl.BlockSpec(memory_space=pl.ANY)] if aliased else []
    return pl.pallas_call(
        functools.partial(tiles_kernel, base, counts, aliased),
        out_shape=jax.ShapeDtypeStruct((8, 2, n_slots, 8, CH_WIN), jnp.bfloat16),
        in_specs=specs,
        out_specs=pl.BlockSpec(memory_space=pl.ANY),
        input_output_aliases={len(operands) - 1: 0} if aliased else {},
        scratch_shapes=[
            pltpu.VMEM((8, 4, 8, CH_WIN), jnp.float32),
            pltpu.VMEM((n, 8, 2, 8, CH_WIN), jnp.bfloat16),
            pltpu.SemaphoreType.DMA((n,)),
        ],
        compiler_params=pltpu.CompilerParams(vmem_limit_bytes=16 * MIB),
        cost_estimate=pl.CostEstimate(flops=n * 5 * 10**7, bytes_accessed=n * 300_000, transcendentals=0),
        name="tiles",
    )(*operands)


def move(array, target):
    places = [(z, y, x) for z in range(N_Z) for y in range(N_Y) for x in range(N_X)]

    def number(z, y, x):
        return (z % N_Z * N_Y + y % N_Y) * N_X + x % N_X

    return lax.ppermute(array, "stn", [(number(*p), number(*target(*p))) for p in places])


def along_z(array, step):
    return move(array, lambda z, y, x: (z + step, y, x))


def across_y(array):
    return move(array, lambda z, y, x: (z, 1 - y, x))


def swap_x(array, mask):
    return move(array, lambda z, y, x: (z, y, x ^ mask))


def per_device(samples, keeper):
    group = lax.axis_index("stn")
    chan = lax.axis_index("chan")
    z, y, x = group // (N_Y * N_X), group // N_X % N_Y, group % N_X
    n_slots = 33

    chan_scalar = chan.astype(jnp.int32).reshape(1)
    pieces = [
        part if d == 0 else lax.ppermute(part, "chan", [(c, (c + d) % 4) for c in range(4)])
        for d, part in enumerate(spectra(samples, chan_scalar))
    ]
    own = group_spectra(pieces, chan_scalar)

    z4, z3, z2, z1 = (along_z(own, step) for step in (4, 3, 2, 1))
    za = jnp.stack([z1, z2])

    def where_from(back, other, mask):
        ry = 1 - y if other else y
        rx = x ^ mask
        if back is None:
            back = jnp.where(ry * N_X + rx < y * N_X + x, 0, 4)
        return ((z - back) % N_Z) * (N_Y * N_X) + ry * N_X + rx

    def froms_a(mask):
        return [(1, 0, mask), (2, 0, mask), (1, 1, mask), (2, 1, mask)]

    froms = [
        [(0, 0, 0)],
        froms_a(0),
        [(3, 0, 0), (4, 0, 0), (3, 1, 0), (None, 1, 0)],
        froms_a(1) + froms_a(3),
        froms_a(2)
        + [(3, 1, 1), (None, 1, 1), (3, 0, 1), (None, 0, 1), (3, 0, 3), (None, 0, 3), (3, 1, 3), (None, 1, 3)],
        [(3, 0, 2), (None, 0, 2), (3, 1, 2), (None, 1, 2)],
    ]
    origin = jnp.stack([where_from(*o) for some in froms for o in some]).astype(jnp.int32)
    keep_row = lax.dynamic_index_in_dim(keeper, group, 0, keepdims=False)
    columns = jnp.arange(keeper.shape[1], dtype=jnp.int32)[None, :]
    rank = jnp.sum(jnp.where(columns < origin[:, None], keep_row[None, :], 0), axis=1)
    kept = jnp.sum(jnp.where(columns == origin[:, None], keep_row[None, :], 0), axis=1)
    slots = jnp.stack([jnp.where(kept == 1, rank, n_slots - 1), kept]).astype(jnp.int32)

    bases = [sum(map(len, froms[:n])) for n in range(len(froms))]

    def add(call, blocks, result):
        return tiles(slots, bases[call], own, blocks, result, n_slots)

    result = add(0, [own[None]], None)
    za, result = lax.optimization_barrier((za, result))
    ya = across_y(za)
    a = jnp.concatenate([za, ya])
    a1, a3 = swap_x(a, 1), swap_x(a, 3)
    result = add(1, [za, ya], result)
    s1, s3, sy = (jnp.where(here, own, z4) for here in (x % 2 == 0, x < 2, y == 0))
    yb = across_y(jnp.stack([z3, sy]))
    yb, result = lax.optimization_barrier((yb, result))
    b1 = swap_x(jnp.concatenate([yb, jnp.stack([z3, s1])]), 1)
    b3 = swap_x(jnp.concatenate([jnp.stack([z3, s3]), yb]), 3)
    result = add(2, [z3[None], z4[None], yb], result)
    a1, a3, result = lax.optimization_barrier((a1, a3, result))
    ar1, ar3 = swap_x(a3[:2], 1), swap_x(a1[2:], 3)
    result = add(3, [a1, a3], result)
    b1, b3, result = lax.optimization_barrier((b1, b3, result))
    br1, br3 = swap_x(b3[:2], 1), swap_x(b1[:2], 3)
    result = add(4, [ar1, ar3, b1, b3], result)
    result = add(5, [br1, br3], result)
    return result.reshape(8, 2, n_slots * 8, CH_WIN).swapaxes(2, 3)


def solution(mesh):
    return jax.shard_map(
        per_device,
        mesh=mesh,
        in_specs=(P(("stn", "chan"), None, None, None), P()),
        out_specs=P("stn", None, "chan", None),
        check_vma=False,
    )
```

```python
import functools
import math

import jax
import jax.numpy as jnp
import numpy as np
from jax import lax
from jax.experimental import pallas as pl
from jax.experimental.pallas import tpu as pltpu
from jax.sharding import PartitionSpec as P

NFFT = 8192
TAPS = 16
CH_WIN = 1024
N_Z, N_Y, N_X = 8, 2, 4
MIB = 1 << 20
UNROLL = 8
SMEM = pltpu.MemorySpace.SMEM
VMEM = pltpu.MemorySpace.VMEM
HBM = pltpu.MemorySpace.HBM


def filter_taps():
    pos = np.arange(TAPS * NFFT, dtype=np.float64)
    shifted = (pos + 0.5) / NFFT - TAPS / 2.0
    window = 0.5 - 0.5 * np.cos(2.0 * math.pi * (pos + 0.5) / (TAPS * NFFT))
    taps = (np.sinc(shifted) * window).reshape(TAPS, 64, 1, 128)
    return np.broadcast_to(taps, (TAPS, 64, 2, 128)).reshape(TAPS, 128, 128).astype(np.float32)


def transform_tables():
    k1 = np.arange(64)
    angle = 2.0 * math.pi * (np.outer(k1, k1) % 64) / 64
    cos, sin = np.cos(angle), np.sin(angle)
    first = np.zeros((2, 64, 64, 2))
    first[0, :, :, 0], first[0, :, :, 1] = cos, sin
    first[1, :, :, 0], first[1, :, :, 1] = -sin, cos
    n2 = np.arange(128)
    turn = 2.0 * math.pi * np.outer(k1, n2) / NFFT
    k2 = np.arange(64)
    angle = 2.0 * math.pi * (np.outer(k2, n2) % 128) / 128
    cos = (np.cos(angle) / math.sqrt(NFFT)).reshape(32, 2, 128).transpose(1, 0, 2)
    sin = (np.sin(angle) / math.sqrt(NFFT)).reshape(32, 2, 128).transpose(1, 0, 2)
    second = np.zeros((2, 2, 32, 2, 128))
    second[:, 0, :, 0], second[:, 0, :, 1] = cos, sin
    second[:, 1, :, 0], second[:, 1, :, 1] = -sin, cos
    return (
        first.reshape(128, 128).astype(np.float32),
        np.stack([np.cos(turn), np.sin(turn)]).astype(np.float32),
        second.reshape(128, 256).astype(np.float32),
    )


def spectra_kernel(*refs):
    chan_ref, outs, held, sems, rows_ref = refs[5], refs[6:10], refs[10:15], refs[15], refs[16]
    copies = [pltpu.make_async_copy(refs[n], held[n], sems.at[n]) for n in range(5)]
    for copy in copies:
        copy.start()
    for copy in copies:
        copy.wait()
    x_ref, taps_ref, first_ref, turn_ref, second_ref = held
    turned = []
    for i in range(2):
        for f in range(2):
            total = taps_ref[0] * x_ref[i, f].astype(jnp.float32)
            for tap in range(1, TAPS):
                total = total + taps_ref[tap] * x_ref[i, f + tap].astype(jnp.float32)
            y = jnp.dot(
                first_ref[...], total, precision=lax.Precision.HIGHEST, preferred_element_type=jnp.float32
            )
            re, im = y[:64], y[64:]
            cos, sin = turn_ref[0], turn_ref[1]
            turned.append(jnp.concatenate([re * cos + im * sin, im * cos - re * sin], axis=1))
    z = jnp.concatenate(turned, axis=0)
    o = lax.dot_general(
        second_ref[...], z, (((1,), (1,)), ((), ())),
        precision=lax.Precision.HIGHEST, preferred_element_type=jnp.float32,
    )
    for p in range(2):
        for i in range(2):
            for f in range(2):
                at = (i * 2 + f) * 64
                even = o[p * 32 : p * 32 + 32, at : at + 64]
                odd = o[64 + p * 32 : 64 + p * 32 + 32, at : at + 64]
                s = jnp.concatenate([even, odd], axis=1)
                row = (p * 2 + f) * 2 + i
                for k in range(32):
                    lane = (k % 8) * 128
                    rows_ref[k // 8, row : row + 1, lane : lane + 128] = s[k : k + 1]
    for d in range(4):
        outs[d][...] = rows_ref[lax.rem(chan_ref[0] + d, 4)].astype(jnp.bfloat16)


def spectra(samples, chan):
    x = samples.reshape(2, 17, 2, 64, 128).transpose(0, 1, 3, 2, 4).reshape(2, 17, 128, 128)
    first, turn, second = transform_tables()
    return pl.pallas_call(
        spectra_kernel,
        out_shape=[jax.ShapeDtypeStruct((8, CH_WIN), jnp.bfloat16)] * 4,
        in_specs=[pl.BlockSpec(memory_space=HBM)] * 5 + [pl.BlockSpec(memory_space=SMEM)],
        out_specs=[pl.BlockSpec(memory_space=VMEM)] * 4,
        scratch_shapes=[
            pltpu.VMEM((2, 17, 128, 128), jnp.bfloat16),
            pltpu.VMEM((TAPS, 128, 128), jnp.float32),
            pltpu.VMEM((128, 128), jnp.float32),
            pltpu.VMEM((2, 64, 128), jnp.float32),
            pltpu.VMEM((128, 256), jnp.float32),
            pltpu.SemaphoreType.DMA((5,)),
            pltpu.VMEM((4, 8, CH_WIN), jnp.float32),
        ],
        compiler_params=pltpu.CompilerParams(vmem_limit_bytes=56 * MIB),
        name="spectra",
    )(x, jnp.asarray(filter_taps()), jnp.asarray(first), jnp.asarray(turn), jnp.asarray(second), chan)


def group_kernel(chan_ref, *refs):
    pieces, out_ref, wide_ref, rows_ref = refs[:4], refs[4], refs[5], refs[6]
    for d in range(4):
        wide_ref[d] = pieces[d][...].astype(jnp.float32)
    for source in range(4):
        piece = wide_ref[lax.rem(chan_ref[0] + 4 - source, 4)]
        for t in range(4):
            rows_ref[t, source * 2 : source * 2 + 2, :] = piece[t * 2 : t * 2 + 2]
    out_ref[...] = rows_ref[...].reshape(32, CH_WIN).astype(jnp.bfloat16)


def group_spectra(pieces, chan):
    return pl.pallas_call(
        group_kernel,
        out_shape=jax.ShapeDtypeStruct((32, CH_WIN), jnp.bfloat16),
        in_specs=[pl.BlockSpec(memory_space=SMEM)] + [pl.BlockSpec(memory_space=VMEM)] * 4,
        out_specs=pl.BlockSpec(memory_space=VMEM),
        scratch_shapes=[pltpu.VMEM((4, 8, CH_WIN), jnp.float32)] * 2,
        compiler_params=pltpu.CompilerParams(vmem_limit_bytes=8 * MIB),
        name="group_spectra",
    )(chan, *pieces)


def tiles_kernel(base, counts, aliased, *refs):
    slots_ref, own_ref = refs[:2]
    blocks = refs[2 : 2 + len(counts)]
    out_ref, wide_ref, tile_ref, sems = refs[2 + len(counts) + (1 if aliased else 0) :]
    own = own_ref[...].astype(jnp.float32) * 0.5
    for t in range(4):
        for i in range(8):
            wide_ref[i, t] = jnp.broadcast_to(own[t * 8 + i : t * 8 + i + 1], (8, CH_WIN))

    def copy_of(n):
        return pltpu.make_async_copy(tile_ref.at[n], out_ref.at[:, :, slots_ref[0, base + n]], sems.at[n])

    first = 0
    for block_ref, count in zip(blocks, counts, strict=True):

        @pl.loop(0, count)
        def _(index, block_ref=block_ref, first=first):
            n = first + index
            keep = slots_ref[1, base + n].astype(jnp.float32)

            @pl.loop(0, CH_WIN // 128, unroll=UNROLL)
            def _(step):
                lanes = pl.ds(pl.multiple_of(step * 128, 128), 128)
                other = block_ref[index, :, lanes].astype(jnp.float32) * keep
                r0, r1, i0, i1 = (other[t * 8 : t * 8 + 8] for t in range(4))
                for i in range(8):
                    a0, a1, b0, b1 = (wide_ref[i, t, :, lanes] for t in range(4))
                    tile_ref[n, i, 0, :, lanes] = ((a0 * r0 + a1 * r1) + (b0 * i0 + b1 * i1)).astype(jnp.bfloat16)
                    tile_ref[n, i, 1, :, lanes] = ((b0 * r0 + b1 * r1) - (a0 * i0 + a1 * i1)).astype(jnp.bfloat16)

            copy_of(n).start()

        first += count

    @pl.loop(0, first)
    def _(n):
        copy_of(n).wait()


def tiles(slots, base, own, blocks, result, n_slots):
    counts = [block.shape[0] for block in blocks]
    n = sum(counts)
    aliased = result is not None
    operands = [slots, own, *blocks] + ([result] if aliased else [])
    specs = [pl.BlockSpec(memory_space=SMEM)] + [pl.BlockSpec(memory_space=VMEM)] * (1 + len(blocks))
    specs += [pl.BlockSpec(memory_space=pl.ANY)] if aliased else []
    return pl.pallas_call(
        functools.partial(tiles_kernel, base, counts, aliased),
        out_shape=jax.ShapeDtypeStruct((8, 2, n_slots, 8, CH_WIN), jnp.bfloat16),
        in_specs=specs,
        out_specs=pl.BlockSpec(memory_space=pl.ANY),
        input_output_aliases={len(operands) - 1: 0} if aliased else {},
        scratch_shapes=[
            pltpu.VMEM((8, 4, 8, CH_WIN), jnp.float32),
            pltpu.VMEM((n, 8, 2, 8, CH_WIN), jnp.bfloat16),
            pltpu.SemaphoreType.DMA((n,)),
        ],
        compiler_params=pltpu.CompilerParams(vmem_limit_bytes=16 * MIB),
        cost_estimate=pl.CostEstimate(flops=n * 10**5, bytes_accessed=n, transcendentals=0),
        name="tiles",
    )(*operands)


def move(array, target):
    places = [(z, y, x) for z in range(N_Z) for y in range(N_Y) for x in range(N_X)]

    def number(z, y, x):
        return (z % N_Z * N_Y + y % N_Y) * N_X + x % N_X

    return lax.ppermute(array, "stn", [(number(*p), number(*target(*p))) for p in places])


def along_z(array, step):
    return move(array, lambda z, y, x: (z + step, y, x))


def across_y(array):
    return move(array, lambda z, y, x: (z, 1 - y, x))


def swap_x(array, mask):
    return move(array, lambda z, y, x: (z, y, x ^ mask))


def per_device(samples, keeper):
    group = lax.axis_index("stn")
    chan = lax.axis_index("chan")
    z, y, x = group // (N_Y * N_X), group // N_X % N_Y, group % N_X
    n_slots = 33

    chan_scalar = chan.astype(jnp.int32).reshape(1)
    pieces = [
        part if d == 0 else lax.ppermute(part, "chan", [(c, (c + d) % 4) for c in range(4)])
        for d, part in enumerate(spectra(samples, chan_scalar))
    ]
    pieces[0] = jnp.where(chan < 4, pieces[0], jnp.zeros((), jnp.bfloat16))
    own = group_spectra(pieces, chan_scalar)

    z3, z2, z1 = (along_z(own, step) for step in (3, 2, 1))
    z4 = along_z(along_z(own, -2), -2)
    za = jnp.stack([z1, z2])

    def where_from(back, other, mask):
        ry = 1 - y if other else y
        rx = x ^ mask
        if back is None:
            back = jnp.where(ry * N_X + rx < y * N_X + x, 0, 4)
        return ((z - back) % N_Z) * (N_Y * N_X) + ry * N_X + rx

    def froms_a(mask):
        return [(1, 0, mask), (2, 0, mask), (1, 1, mask), (2, 1, mask)]

    froms = [
        [(0, 0, 0)] + froms_a(0) + [(3, 0, 0), (4, 0, 0), (3, 1, 0), (None, 1, 0)],
        froms_a(1) + froms_a(3),
        froms_a(2)
        + [(3, 1, 1), (None, 1, 1), (3, 0, 1), (None, 0, 1), (3, 0, 3), (None, 0, 3), (3, 1, 3), (None, 1, 3)],
        [(3, 0, 2), (None, 0, 2), (3, 1, 2), (None, 1, 2)],
    ]
    origin = jnp.stack([where_from(*o) for some in froms for o in some]).astype(jnp.int32)
    keep_row = lax.dynamic_index_in_dim(keeper, group, 0, keepdims=False)
    columns = jnp.arange(keeper.shape[1], dtype=jnp.int32)[None, :]
    rank = jnp.sum(jnp.where(columns < origin[:, None], keep_row[None, :], 0), axis=1)
    kept = jnp.sum(jnp.where(columns == origin[:, None], keep_row[None, :], 0), axis=1)
    slots = jnp.stack([jnp.where(kept == 1, rank, n_slots - 1), kept]).astype(jnp.int32)

    bases = [sum(map(len, froms[:n])) for n in range(len(froms))]

    def add(call, blocks, result):
        return tiles(slots, bases[call], own, blocks, result, n_slots)

    ya = across_y(za)
    a = jnp.concatenate([za, ya])
    a1, a3 = swap_x(a, 1), swap_x(a, 3)
    s1, s3, sy = (jnp.where(here, own, z4) for here in (x % 2 == 0, x < 2, y == 0))
    yb = across_y(jnp.stack([z3, sy]))
    b1 = swap_x(jnp.concatenate([yb, jnp.stack([z3, s1])]), 1)
    b3 = swap_x(jnp.concatenate([jnp.stack([z3, s3]), yb]), 3)
    result = add(0, [own[None], za, ya, z3[None], z4[None], yb], None)
    a1, a3, result = lax.optimization_barrier((a1, a3, result))
    ar1, ar3 = swap_x(a3[:2], 1), swap_x(a1[2:], 3)
    result = add(1, [a1, a3], result)
    b1, b3, result = lax.optimization_barrier((b1, b3, result))
    br1, br3 = swap_x(b3[:2], 1), swap_x(b1[:2], 3)
    result = add(2, [ar1, ar3, b1, b3], result)
    result = add(3, [br1, br3], result)
    return result.reshape(8, 2, n_slots * 8, CH_WIN).swapaxes(2, 3)


def solution(mesh):
    return jax.shard_map(
        per_device,
        mesh=mesh,
        in_specs=(P(("stn", "chan"), None, None, None), P()),
        out_specs=P("stn", None, "chan", None),
        check_vma=False,
    )
```

```python
import functools
import math

import jax
import jax.numpy as jnp
import numpy as np
from jax import lax
from jax.experimental import pallas as pl
from jax.experimental.pallas import tpu as pltpu
from jax.sharding import PartitionSpec as P

NFFT = 8192
TAPS = 16
CH_WIN = 1024
N_Z, N_Y, N_X = 8, 2, 4
MIB = 1 << 20
UNROLL = 8
FRAME_CUTS = ((0, 5), (5, 9), (9, 13), (13, 17))
SMEM = pltpu.MemorySpace.SMEM
VMEM = pltpu.MemorySpace.VMEM
HBM = pltpu.MemorySpace.HBM


def filter_taps():
    pos = np.arange(TAPS * NFFT, dtype=np.float64)
    shifted = (pos + 0.5) / NFFT - TAPS / 2.0
    window = 0.5 - 0.5 * np.cos(2.0 * math.pi * (pos + 0.5) / (TAPS * NFFT))
    taps = (np.sinc(shifted) * window).reshape(TAPS, 64, 1, 128)
    return np.broadcast_to(taps, (TAPS, 64, 2, 128)).reshape(TAPS, 128, 128).astype(np.float32)


def transform_tables():
    k1 = np.arange(64)
    angle = 2.0 * math.pi * (np.outer(k1, k1) % 64) / 64
    cos, sin = np.cos(angle), np.sin(angle)
    first = np.zeros((2, 64, 64, 2))
    first[0, :, :, 0], first[0, :, :, 1] = cos, sin
    first[1, :, :, 0], first[1, :, :, 1] = -sin, cos
    n2 = np.arange(128)
    turn = 2.0 * math.pi * np.outer(k1, n2) / NFFT
    k2 = np.arange(64)
    angle = 2.0 * math.pi * (np.outer(k2, n2) % 128) / 128
    cos = (np.cos(angle) / math.sqrt(NFFT)).reshape(32, 2, 128).transpose(1, 0, 2)
    sin = (np.sin(angle) / math.sqrt(NFFT)).reshape(32, 2, 128).transpose(1, 0, 2)
    second = np.zeros((2, 2, 32, 2, 128))
    second[:, 0, :, 0], second[:, 0, :, 1] = cos, sin
    second[:, 1, :, 0], second[:, 1, :, 1] = -sin, cos
    return (
        first.reshape(128, 128).astype(np.float32),
        np.stack([np.cos(turn), np.sin(turn)]).astype(np.float32),
        second.reshape(128, 256).astype(np.float32),
    )


def spectra_kernel(*refs):
    sources, chan_ref, outs, held, sems, total_ref, rows_ref = refs[:5], refs[5], refs[6:10], refs[10:15], *refs[15:]
    x_ref, taps_ref, first_ref, turn_ref, second_ref = held
    copies = []
    for n, (low, high) in enumerate(FRAME_CUTS):
        frames, taps = pl.ds(low, high - low), pl.ds(low, min(high, TAPS) - low)
        copies.append(pltpu.make_async_copy(sources[0].at[:, frames], x_ref.at[:, frames], sems.at[2 * n]))
        copies.append(pltpu.make_async_copy(sources[1].at[taps], taps_ref.at[taps], sems.at[2 * n + 1]))
    cut = len(copies)
    copies += [pltpu.make_async_copy(sources[n], held[n], sems.at[cut + n - 2]) for n in range(2, 5)]
    for copy in copies:
        copy.start()
    for n, (low, high) in enumerate(FRAME_CUTS):
        copies[2 * n].wait()
        copies[2 * n + 1].wait()
        for i in range(2):
            for f in range(2):
                terms = [
                    taps_ref[frame - f] * x_ref[i, frame].astype(jnp.float32)
                    for frame in range(low, high)
                    if 0 <= frame - f < TAPS
                ]
                total = functools.reduce(jnp.add, terms)
                total_ref[i * 2 + f] = total if n == 0 else total_ref[i * 2 + f] + total
    for copy in copies[cut:]:
        copy.wait()
    turned = []
    for i in range(2):
        for f in range(2):
            total = total_ref[i * 2 + f]
            y = jnp.dot(
                first_ref[...], total, precision=lax.Precision.HIGHEST, preferred_element_type=jnp.float32
            )
            re, im = y[:64], y[64:]
            cos, sin = turn_ref[0], turn_ref[1]
            turned.append(jnp.concatenate([re * cos + im * sin, im * cos - re * sin], axis=1))
    z = jnp.concatenate(turned, axis=0)
    o = lax.dot_general(
        second_ref[...], z, (((1,), (1,)), ((), ())),
        precision=lax.Precision.HIGHEST, preferred_element_type=jnp.float32,
    )
    for p in range(2):
        for i in range(2):
            for f in range(2):
                at = (i * 2 + f) * 64
                even = o[p * 32 : p * 32 + 32, at : at + 64]
                odd = o[64 + p * 32 : 64 + p * 32 + 32, at : at + 64]
                s = jnp.concatenate([even, odd], axis=1)
                row = (p * 2 + f) * 2 + i
                for k in range(32):
                    lane = (k % 8) * 128
                    rows_ref[k // 8, row : row + 1, lane : lane + 128] = s[k : k + 1]
    for d in range(4):
        outs[d][...] = rows_ref[lax.bitwise_xor(chan_ref[0], d)].astype(jnp.bfloat16)


def spectra(samples, chan):
    x = samples.reshape(2, 17, 2, 64, 128).transpose(0, 1, 3, 2, 4).reshape(2, 17, 128, 128)
    first, turn, second = transform_tables()
    return pl.pallas_call(
        spectra_kernel,
        out_shape=[jax.ShapeDtypeStruct((8, CH_WIN), jnp.bfloat16)] * 4,
        in_specs=[pl.BlockSpec(memory_space=HBM)] * 5 + [pl.BlockSpec(memory_space=SMEM)],
        out_specs=[pl.BlockSpec(memory_space=VMEM)] * 4,
        scratch_shapes=[
            pltpu.VMEM((2, 17, 128, 128), jnp.bfloat16),
            pltpu.VMEM((TAPS, 128, 128), jnp.float32),
            pltpu.VMEM((128, 128), jnp.float32),
            pltpu.VMEM((2, 64, 128), jnp.float32),
            pltpu.VMEM((128, 256), jnp.float32),
            pltpu.SemaphoreType.DMA((2 * len(FRAME_CUTS) + 3,)),
            pltpu.VMEM((4, 128, 128), jnp.float32),
            pltpu.VMEM((4, 8, CH_WIN), jnp.float32),
        ],
        compiler_params=pltpu.CompilerParams(vmem_limit_bytes=56 * MIB),
        name="spectra",
    )(x, jnp.asarray(filter_taps()), jnp.asarray(first), jnp.asarray(turn), jnp.asarray(second), chan)


def group_kernel(chan_ref, *refs):
    pieces, out_ref, wide_ref, rows_ref = refs[:4], refs[4], refs[5], refs[6]
    for d in range(4):
        wide_ref[d] = pieces[d][...].astype(jnp.float32)
    for source in range(4):
        piece = wide_ref[lax.bitwise_xor(chan_ref[0], source)]
        for t in range(4):
            rows_ref[t, source * 2 : source * 2 + 2, :] = piece[t * 2 : t * 2 + 2]
    out_ref[...] = rows_ref[...].reshape(32, CH_WIN).astype(jnp.bfloat16)


def group_spectra(pieces, chan):
    return pl.pallas_call(
        group_kernel,
        out_shape=jax.ShapeDtypeStruct((32, CH_WIN), jnp.bfloat16),
        in_specs=[pl.BlockSpec(memory_space=SMEM)] + [pl.BlockSpec(memory_space=VMEM)] * 4,
        out_specs=pl.BlockSpec(memory_space=VMEM),
        scratch_shapes=[pltpu.VMEM((4, 8, CH_WIN), jnp.float32)] * 2,
        compiler_params=pltpu.CompilerParams(vmem_limit_bytes=8 * MIB),
        name="group_spectra",
    )(chan, *pieces)


def tiles_kernel(base, counts, aliased, *refs):
    slots_ref, own_ref = refs[:2]
    blocks = refs[2 : 2 + len(counts)]
    out_ref, wide_ref, tile_ref, sems = refs[2 + len(counts) + (1 if aliased else 0) :]
    own = own_ref[...].astype(jnp.float32) * 0.5
    for t in range(4):
        for i in range(8):
            wide_ref[i, t] = jnp.broadcast_to(own[t * 8 + i : t * 8 + i + 1], (8, CH_WIN))

    def copy_of(n):
        return pltpu.make_async_copy(tile_ref.at[n], out_ref.at[:, :, slots_ref[0, base + n]], sems.at[n])

    first = 0
    for block_ref, count in zip(blocks, counts, strict=True):

        @pl.loop(0, count)
        def _(index, block_ref=block_ref, first=first):
            n = first + index
            keep = slots_ref[1, base + n].astype(jnp.float32)

            @pl.loop(0, CH_WIN // 128, unroll=UNROLL)
            def _(step):
                lanes = pl.ds(pl.multiple_of(step * 128, 128), 128)
                other = block_ref[index, :, lanes].astype(jnp.float32) * keep
                r0, r1, i0, i1 = (other[t * 8 : t * 8 + 8] for t in range(4))
                for i in range(8):
                    a0, a1, b0, b1 = (wide_ref[i, t, :, lanes] for t in range(4))
                    tile_ref[n, i, 0, :, lanes] = ((a0 * r0 + a1 * r1) + (b0 * i0 + b1 * i1)).astype(jnp.bfloat16)
                    tile_ref[n, i, 1, :, lanes] = ((b0 * r0 + b1 * r1) - (a0 * i0 + a1 * i1)).astype(jnp.bfloat16)

            copy_of(n).start()

        first += count

    @pl.loop(0, first)
    def _(n):
        copy_of(n).wait()


def tiles(slots, base, own, blocks, result, n_slots):
    counts = [block.shape[0] for block in blocks]
    n = sum(counts)
    aliased = result is not None
    operands = [slots, own, *blocks] + ([result] if aliased else [])
    specs = [pl.BlockSpec(memory_space=SMEM)] + [pl.BlockSpec(memory_space=VMEM)] * (1 + len(blocks))
    specs += [pl.BlockSpec(memory_space=pl.ANY)] if aliased else []
    return pl.pallas_call(
        functools.partial(tiles_kernel, base, counts, aliased),
        out_shape=jax.ShapeDtypeStruct((8, 2, n_slots, 8, CH_WIN), jnp.bfloat16),
        in_specs=specs,
        out_specs=pl.BlockSpec(memory_space=pl.ANY),
        input_output_aliases={len(operands) - 1: 0} if aliased else {},
        scratch_shapes=[
            pltpu.VMEM((8, 4, 8, CH_WIN), jnp.float32),
            pltpu.VMEM((n, 8, 2, 8, CH_WIN), jnp.bfloat16),
            pltpu.SemaphoreType.DMA((n,)),
        ],
        compiler_params=pltpu.CompilerParams(vmem_limit_bytes=16 * MIB),
        cost_estimate=pl.CostEstimate(flops=n * 10**5, bytes_accessed=n, transcendentals=0),
        name="tiles",
    )(*operands)


def move(array, target):
    places = [(z, y, x) for z in range(N_Z) for y in range(N_Y) for x in range(N_X)]

    def number(z, y, x):
        return (z % N_Z * N_Y + y % N_Y) * N_X + x % N_X

    return lax.ppermute(array, "stn", [(number(*p), number(*target(*p))) for p in places])


def along_z(array, step):
    return move(array, lambda z, y, x: (z + step, y, x))


def across_y(array):
    return move(array, lambda z, y, x: (z, 1 - y, x))


def swap_x(array, mask):
    return move(array, lambda z, y, x: (z, y, x ^ mask))


def per_device(samples, keeper):
    group = lax.axis_index("stn")
    chan = lax.axis_index("chan")
    z, y, x = group // (N_Y * N_X), group // N_X % N_Y, group % N_X
    n_slots = 33

    chan_scalar = chan.astype(jnp.int32).reshape(1)
    pieces = [
        part if d == 0 else lax.ppermute(part, "chan", [(c, c ^ d) for c in range(4)])
        for d, part in enumerate(spectra(samples, chan_scalar))
    ]
    pieces[0] = jnp.where(chan < 4, pieces[0], jnp.zeros((), jnp.bfloat16))
    own = group_spectra(pieces, chan_scalar)

    z3, z2, z1 = (along_z(own, step) for step in (3, 2, 1))
    z4 = along_z(along_z(own, -2), -2)
    za = jnp.stack([z1, z2])

    def where_from(back, other, mask):
        ry = 1 - y if other else y
        rx = x ^ mask
        if back is None:
            back = jnp.where(ry * N_X + rx < y * N_X + x, 0, 4)
        return ((z - back) % N_Z) * (N_Y * N_X) + ry * N_X + rx

    def froms_a(mask):
        return [(1, 0, mask), (2, 0, mask), (1, 1, mask), (2, 1, mask)]

    froms = [
        [(0, 0, 0)] + froms_a(0) + [(3, 0, 0), (4, 0, 0), (3, 1, 0), (None, 1, 0)],
        froms_a(1) + froms_a(3),
        froms_a(2)
        + [(3, 1, 1), (None, 1, 1), (3, 0, 1), (None, 0, 1), (3, 0, 3), (None, 0, 3), (3, 1, 3), (None, 1, 3)],
        [(3, 0, 2), (None, 0, 2), (3, 1, 2), (None, 1, 2)],
    ]
    origin = jnp.stack([where_from(*o) for some in froms for o in some]).astype(jnp.int32)
    keep_row = lax.dynamic_index_in_dim(keeper, group, 0, keepdims=False)
    columns = jnp.arange(keeper.shape[1], dtype=jnp.int32)[None, :]
    rank = jnp.sum(jnp.where(columns < origin[:, None], keep_row[None, :], 0), axis=1)
    kept = jnp.sum(jnp.where(columns == origin[:, None], keep_row[None, :], 0), axis=1)
    slots = jnp.stack([jnp.where(kept == 1, rank, n_slots - 1), kept]).astype(jnp.int32)

    bases = [sum(map(len, froms[:n])) for n in range(len(froms))]

    def add(call, blocks, result):
        return tiles(slots, bases[call], own, blocks, result, n_slots)

    ya = across_y(za)
    a = jnp.concatenate([za, ya])
    a1, a3 = swap_x(a, 1), swap_x(a, 3)
    s1, s3, sy = (jnp.where(here, own, z4) for here in (x % 2 == 0, x < 2, y == 0))
    yb = across_y(jnp.stack([z3, sy]))
    b1 = swap_x(jnp.concatenate([yb, jnp.stack([z3, s1])]), 1)
    b3 = swap_x(jnp.concatenate([jnp.stack([z3, s3]), yb]), 3)
    result = add(0, [own[None], za, ya, z3[None], z4[None], yb], None)
    a1, a3, result = lax.optimization_barrier((a1, a3, result))
    ar1, ar3 = swap_x(a3[:2], 1), swap_x(a1[2:], 3)
    result = add(1, [a1, a3], result)
    b1, b3, result = lax.optimization_barrier((b1, b3, result))
    br1, br3 = swap_x(b3[:2], 1), swap_x(b1[:2], 3)
    result = add(2, [ar1, ar3, b1, b3], result)
    result = add(3, [br1, br3], result)
    return result.reshape(8, 2, n_slots * 8, CH_WIN).swapaxes(2, 3)


def solution(mesh):
    return jax.shard_map(
        per_device,
        mesh=mesh,
        in_specs=(P(("stn", "chan"), None, None, None), P()),
        out_specs=P("stn", None, "chan", None),
        check_vma=False,
    )
```

```python
import functools
import math

import jax
import jax.numpy as jnp
import numpy as np
from jax import lax
from jax.experimental import pallas as pl
from jax.experimental.pallas import tpu as pltpu
from jax.sharding import PartitionSpec as P

NFFT = 8192
TAPS = 16
CH_WIN = 1024
N_Z, N_Y, N_X = 8, 2, 4
MIB = 1 << 20
UNROLL = 8
FRAME_CUTS = ((0, 5), (5, 9), (9, 13), (13, 17))
SMEM = pltpu.MemorySpace.SMEM
VMEM = pltpu.MemorySpace.VMEM
HBM = pltpu.MemorySpace.HBM


def filter_taps():
    pos = np.arange(TAPS * NFFT, dtype=np.float64)
    shifted = (pos + 0.5) / NFFT - TAPS / 2.0
    window = 0.5 - 0.5 * np.cos(2.0 * math.pi * (pos + 0.5) / (TAPS * NFFT))
    taps = (np.sinc(shifted) * window).reshape(TAPS, 64, 1, 128)
    return np.broadcast_to(taps, (TAPS, 64, 2, 128)).reshape(TAPS, 128, 128).astype(np.float32)


def transform_tables():
    k1 = np.arange(64)
    angle = 2.0 * math.pi * (np.outer(k1, k1) % 64) / 64
    cos, sin = np.cos(angle), np.sin(angle)
    first = np.zeros((2, 64, 64, 2))
    first[0, :, :, 0], first[0, :, :, 1] = cos, sin
    first[1, :, :, 0], first[1, :, :, 1] = -sin, cos
    n2 = np.arange(128)
    turn = 2.0 * math.pi * np.outer(k1, n2) / NFFT
    k2 = np.arange(64)
    angle = 2.0 * math.pi * (np.outer(k2, n2) % 128) / 128
    cos = (np.cos(angle) / math.sqrt(NFFT)).reshape(32, 2, 128).transpose(1, 0, 2)
    sin = (np.sin(angle) / math.sqrt(NFFT)).reshape(32, 2, 128).transpose(1, 0, 2)
    second = np.zeros((2, 2, 32, 2, 128))
    second[:, 0, :, 0], second[:, 0, :, 1] = cos, sin
    second[:, 1, :, 0], second[:, 1, :, 1] = -sin, cos
    return (
        first.reshape(128, 128).astype(np.float32),
        np.stack([np.cos(turn), np.sin(turn)]).astype(np.float32),
        second.reshape(128, 256).astype(np.float32),
    )


def spectra_kernel(*refs):
    sources, chan_ref, outs, held, sems, total_ref, rows_ref = refs[:5], refs[5], refs[6:10], refs[10:15], *refs[15:]
    x_ref, taps_ref, first_ref, turn_ref, second_ref = held
    copies = []
    for n, (low, high) in enumerate(FRAME_CUTS):
        frames, taps = pl.ds(low, high - low), pl.ds(low, min(high, TAPS) - low)
        copies.append(pltpu.make_async_copy(sources[0].at[:, frames], x_ref.at[:, frames], sems.at[2 * n]))
        copies.append(pltpu.make_async_copy(sources[1].at[taps], taps_ref.at[taps], sems.at[2 * n + 1]))
    cut = len(copies)
    copies += [pltpu.make_async_copy(sources[n], held[n], sems.at[cut + n - 2]) for n in range(2, 5)]
    for copy in copies:
        copy.start()
    for n, (low, high) in enumerate(FRAME_CUTS):
        copies[2 * n].wait()
        copies[2 * n + 1].wait()
        for i in range(2):
            for f in range(2):
                terms = [
                    taps_ref[frame - f] * x_ref[i, frame].astype(jnp.float32)
                    for frame in range(low, high)
                    if 0 <= frame - f < TAPS
                ]
                total = functools.reduce(jnp.add, terms)
                total_ref[i * 2 + f] = total if n == 0 else total_ref[i * 2 + f] + total
    for copy in copies[cut:]:
        copy.wait()
    turned = []
    for i in range(2):
        for f in range(2):
            total = total_ref[i * 2 + f]
            y = jnp.dot(
                first_ref[...], total, precision=lax.Precision.HIGHEST, preferred_element_type=jnp.float32
            )
            re, im = y[:64], y[64:]
            cos, sin = turn_ref[0], turn_ref[1]
            turned.append(jnp.concatenate([re * cos + im * sin, im * cos - re * sin], axis=1))
    z = jnp.concatenate(turned, axis=0)
    o = lax.dot_general(
        second_ref[...], z, (((1,), (1,)), ((), ())),
        precision=lax.Precision.HIGHEST, preferred_element_type=jnp.float32,
    )
    for p in range(2):
        for i in range(2):
            for f in range(2):
                at = (i * 2 + f) * 64
                even = o[p * 32 : p * 32 + 32, at : at + 64]
                odd = o[64 + p * 32 : 64 + p * 32 + 32, at : at + 64]
                s = jnp.concatenate([even, odd], axis=1)
                row = (p * 2 + f) * 2 + i
                for k in range(32):
                    lane = (k % 8) * 128
                    rows_ref[k // 8, row : row + 1, lane : lane + 128] = s[k : k + 1]
    for d in range(4):
        outs[d][...] = rows_ref[lax.bitwise_xor(chan_ref[0], d)].astype(jnp.bfloat16)


def spectra(samples, chan):
    x = samples.reshape(2, 17, 2, 64, 128).transpose(0, 1, 3, 2, 4).reshape(2, 17, 128, 128)
    first, turn, second = transform_tables()
    return pl.pallas_call(
        spectra_kernel,
        out_shape=[jax.ShapeDtypeStruct((8, CH_WIN), jnp.bfloat16)] * 4,
        in_specs=[pl.BlockSpec(memory_space=HBM)] * 5 + [pl.BlockSpec(memory_space=SMEM)],
        out_specs=[pl.BlockSpec(memory_space=VMEM)] * 4,
        scratch_shapes=[
            pltpu.VMEM((2, 17, 128, 128), jnp.bfloat16),
            pltpu.VMEM((TAPS, 128, 128), jnp.float32),
            pltpu.VMEM((128, 128), jnp.float32),
            pltpu.VMEM((2, 64, 128), jnp.float32),
            pltpu.VMEM((128, 256), jnp.float32),
            pltpu.SemaphoreType.DMA((2 * len(FRAME_CUTS) + 3,)),
            pltpu.VMEM((4, 128, 128), jnp.float32),
            pltpu.VMEM((4, 8, CH_WIN), jnp.float32),
        ],
        compiler_params=pltpu.CompilerParams(vmem_limit_bytes=56 * MIB),
        name="spectra",
    )(x, jnp.asarray(filter_taps()), jnp.asarray(first), jnp.asarray(turn), jnp.asarray(second), chan)


def group_kernel(chan_ref, *refs):
    pieces, out_ref, wide_ref, rows_ref = refs[:4], refs[4], refs[5], refs[6]
    for d in range(4):
        wide_ref[d] = pieces[d][...].astype(jnp.float32)
    for source in range(4):
        piece = wide_ref[lax.bitwise_xor(chan_ref[0], source)]
        for t in range(4):
            rows_ref[t, source * 2 : source * 2 + 2, :] = piece[t * 2 : t * 2 + 2]
    out_ref[...] = rows_ref[...].reshape(32, CH_WIN).astype(jnp.bfloat16)


def group_spectra(pieces, chan):
    return pl.pallas_call(
        group_kernel,
        out_shape=jax.ShapeDtypeStruct((32, CH_WIN), jnp.bfloat16),
        in_specs=[pl.BlockSpec(memory_space=SMEM)] + [pl.BlockSpec(memory_space=VMEM)] * 4,
        out_specs=pl.BlockSpec(memory_space=VMEM),
        scratch_shapes=[pltpu.VMEM((4, 8, CH_WIN), jnp.float32)] * 2,
        compiler_params=pltpu.CompilerParams(vmem_limit_bytes=8 * MIB),
        name="group_spectra",
    )(chan, *pieces)


def tiles_kernel(base, counts, aliased, *refs):
    slots_ref, own_ref = refs[:2]
    blocks = refs[2 : 2 + len(counts)]
    out_ref, wide_ref, tile_ref, sems = refs[2 + len(counts) + (1 if aliased else 0) :]
    own = own_ref[...].astype(jnp.float32) * 0.5
    for t in range(4):
        for i in range(8):
            wide_ref[i, t] = jnp.broadcast_to(own[t * 8 + i : t * 8 + i + 1], (8, CH_WIN))

    def copy_of(n):
        return pltpu.make_async_copy(tile_ref.at[n], out_ref.at[:, :, slots_ref[0, base + n]], sems.at[n])

    first = 0
    for block_ref, count in zip(blocks, counts, strict=True):

        @pl.loop(0, count)
        def _(index, block_ref=block_ref, first=first):
            n = first + index
            keep = slots_ref[1, base + n].astype(jnp.float32)

            @pl.loop(0, CH_WIN // 128, unroll=UNROLL)
            def _(step):
                lanes = pl.ds(pl.multiple_of(step * 128, 128), 128)
                other = block_ref[index, :, lanes].astype(jnp.float32) * keep
                r0, r1, i0, i1 = (other[t * 8 : t * 8 + 8] for t in range(4))
                for i in range(8):
                    a0, a1, b0, b1 = (wide_ref[i, t, :, lanes] for t in range(4))
                    tile_ref[n, i, 0, :, lanes] = ((a0 * r0 + a1 * r1) + (b0 * i0 + b1 * i1)).astype(jnp.bfloat16)
                    tile_ref[n, i, 1, :, lanes] = ((b0 * r0 + b1 * r1) - (a0 * i0 + a1 * i1)).astype(jnp.bfloat16)

            copy_of(n).start()

        first += count

    @pl.loop(0, first)
    def _(n):
        copy_of(n).wait()


def tiles(slots, base, own, blocks, result, n_slots):
    counts = [block.shape[0] for block in blocks]
    n = sum(counts)
    aliased = result is not None
    operands = [slots, own, *blocks] + ([result] if aliased else [])
    specs = [pl.BlockSpec(memory_space=SMEM)] + [pl.BlockSpec(memory_space=VMEM)] * (1 + len(blocks))
    specs += [pl.BlockSpec(memory_space=pl.ANY)] if aliased else []
    return pl.pallas_call(
        functools.partial(tiles_kernel, base, counts, aliased),
        out_shape=jax.ShapeDtypeStruct((8, 2, n_slots, 8, CH_WIN), jnp.bfloat16),
        in_specs=specs,
        out_specs=pl.BlockSpec(memory_space=pl.ANY),
        input_output_aliases={len(operands) - 1: 0} if aliased else {},
        scratch_shapes=[
            pltpu.VMEM((8, 4, 8, CH_WIN), jnp.float32),
            pltpu.VMEM((n, 8, 2, 8, CH_WIN), jnp.bfloat16),
            pltpu.SemaphoreType.DMA((n,)),
        ],
        compiler_params=pltpu.CompilerParams(vmem_limit_bytes=16 * MIB),
        cost_estimate=pl.CostEstimate(flops=n * 10**5, bytes_accessed=n, transcendentals=0),
        name="tiles",
    )(*operands)


def move(array, target):
    places = [(z, y, x) for z in range(N_Z) for y in range(N_Y) for x in range(N_X)]

    def number(z, y, x):
        return (z % N_Z * N_Y + y % N_Y) * N_X + x % N_X

    return lax.ppermute(array, "stn", [(number(*p), number(*target(*p))) for p in places])


def along_z(array, step):
    return move(array, lambda z, y, x: (z + step, y, x))


def across_y(array):
    return move(array, lambda z, y, x: (z, 1 - y, x))


def swap_x(array, mask):
    return move(array, lambda z, y, x: (z, y, x ^ mask))


def per_device(samples, keeper):
    group = lax.axis_index("stn")
    chan = lax.axis_index("chan")
    z, y, x = group // (N_Y * N_X), group // N_X % N_Y, group % N_X
    n_slots = 33

    chan_scalar = chan.astype(jnp.int32).reshape(1)
    pieces = [
        part if d == 0 else lax.ppermute(part, "chan", [(c, c ^ d) for c in range(4)])
        for d, part in enumerate(spectra(samples, chan_scalar))
    ]
    pieces[0] = jnp.where(chan < 4, pieces[0], jnp.zeros((), jnp.bfloat16))
    own = group_spectra(pieces, chan_scalar)

    z3, z2, z1 = (along_z(own, step) for step in (3, 2, 1))
    z4 = along_z(along_z(own, -2), -2)
    za = jnp.stack([z1, z2])

    def where_from(back, other, mask):
        ry = 1 - y if other else y
        rx = x ^ mask
        if back is None:
            back = jnp.where(ry * N_X + rx < y * N_X + x, 0, 4)
        return ((z - back) % N_Z) * (N_Y * N_X) + ry * N_X + rx

    def froms_a(other):
        return [(back, other, mask) for mask in (0, 1, 3, 2) for back in (1, 2)]

    froms = [
        [(0, 0, 0)] + froms_a(0) + [(3, 0, 0), (4, 0, 0), (3, 1, 0), (None, 1, 0)],
        [(3, 1, 1), (None, 1, 1), (3, 0, 1), (None, 0, 1), (3, 0, 3), (None, 0, 3), (3, 1, 3), (None, 1, 3)],
        froms_a(1) + [(3, 0, 2), (None, 0, 2), (3, 1, 2), (None, 1, 2)],
    ]
    origin = jnp.stack([where_from(*o) for some in froms for o in some]).astype(jnp.int32)
    keep_row = lax.dynamic_index_in_dim(keeper, group, 0, keepdims=False)
    columns = jnp.arange(keeper.shape[1], dtype=jnp.int32)[None, :]
    rank = jnp.sum(jnp.where(columns < origin[:, None], keep_row[None, :], 0), axis=1)
    kept = jnp.sum(jnp.where(columns == origin[:, None], keep_row[None, :], 0), axis=1)
    slots = jnp.stack([jnp.where(kept == 1, rank, n_slots - 1), kept]).astype(jnp.int32)

    bases = [sum(map(len, froms[:n])) for n in range(len(froms))]

    def add(call, blocks, result):
        return tiles(slots, bases[call], own, blocks, result, n_slots)

    a1, a3 = swap_x(za, 1), swap_x(za, 3)
    ar1, ar3 = swap_x(a3[:1], 1), swap_x(a1[1:], 3)
    s1, s3, sy = (jnp.where(here, own, z4) for here in (x % 2 == 0, x < 2, y == 0))
    yb = across_y(jnp.stack([z3, sy]))
    row = jnp.concatenate([za, a1, a3, ar1, ar3])
    ya = across_y(row)
    b1 = swap_x(jnp.concatenate([yb, jnp.stack([z3, s1])]), 1)
    b3 = swap_x(jnp.concatenate([jnp.stack([z3, s3]), yb]), 3)
    result = add(0, [own[None], row, z3[None], z4[None], yb], None)
    b1, b3, result = lax.optimization_barrier((b1, b3, result))
    br1, br3 = swap_x(b3[:2], 1), swap_x(b1[:2], 3)
    result = add(1, [b1, b3], result)
    result = add(2, [ya, br1, br3], result)
    return result.reshape(8, 2, n_slots * 8, CH_WIN).swapaxes(2, 3)


def solution(mesh):
    return jax.shard_map(
        per_device,
        mesh=mesh,
        in_specs=(P(("stn", "chan"), None, None, None), P()),
        out_specs=P("stn", None, "chan", None),
        check_vma=False,
    )
```

```python
import functools
import math

import jax
import jax.numpy as jnp
import numpy as np
from jax import lax
from jax.experimental import pallas as pl
from jax.experimental.pallas import tpu as pltpu
from jax.sharding import PartitionSpec as P

NFFT = 8192
TAPS = 16
CH_WIN = 1024
N_Z, N_Y, N_X = 8, 2, 4
MIB = 1 << 20
UNROLL = 8
FRAME_CUTS = ((0, 5), (5, 9), (9, 13), (13, 17))
SMEM = pltpu.MemorySpace.SMEM
VMEM = pltpu.MemorySpace.VMEM
HBM = pltpu.MemorySpace.HBM


def filter_taps():
    pos = np.arange(TAPS * NFFT, dtype=np.float64)
    shifted = (pos + 0.5) / NFFT - TAPS / 2.0
    window = 0.5 - 0.5 * np.cos(2.0 * math.pi * (pos + 0.5) / (TAPS * NFFT))
    taps = (np.sinc(shifted) * window).reshape(TAPS, 64, 1, 128)
    return np.broadcast_to(taps, (TAPS, 64, 2, 128)).reshape(TAPS, 128, 128).astype(np.float32)


def transform_tables():
    k1 = np.arange(64)
    angle = 2.0 * math.pi * (np.outer(k1, k1) % 64) / 64
    cos, sin = np.cos(angle), np.sin(angle)
    first = np.zeros((2, 64, 64, 2))
    first[0, :, :, 0], first[0, :, :, 1] = cos, sin
    first[1, :, :, 0], first[1, :, :, 1] = -sin, cos
    n2 = np.arange(128)
    turn = 2.0 * math.pi * np.outer(k1, n2) / NFFT
    k2 = np.arange(64)
    angle = 2.0 * math.pi * (np.outer(k2, n2) % 128) / 128
    cos = (np.cos(angle) / math.sqrt(NFFT)).reshape(32, 2, 128).transpose(1, 0, 2)
    sin = (np.sin(angle) / math.sqrt(NFFT)).reshape(32, 2, 128).transpose(1, 0, 2)
    second = np.zeros((2, 2, 32, 2, 128))
    second[:, 0, :, 0], second[:, 0, :, 1] = cos, sin
    second[:, 1, :, 0], second[:, 1, :, 1] = -sin, cos
    return (
        first.reshape(128, 128).astype(np.float32),
        np.stack([np.cos(turn), np.sin(turn)]).astype(np.float32),
        second.reshape(128, 256).astype(np.float32),
    )


def spectra_kernel(*refs):
    sources, chan_ref, outs, held, sems, total_ref, rows_ref = refs[:5], refs[5], refs[6:10], refs[10:15], *refs[15:]
    x_ref, taps_ref, first_ref, turn_ref, second_ref = held
    copies = []
    for n, (low, high) in enumerate(FRAME_CUTS):
        frames, taps = pl.ds(low, high - low), pl.ds(low, min(high, TAPS) - low)
        copies.append(pltpu.make_async_copy(sources[0].at[:, frames], x_ref.at[:, frames], sems.at[2 * n]))
        copies.append(pltpu.make_async_copy(sources[1].at[taps], taps_ref.at[taps], sems.at[2 * n + 1]))
    cut = len(copies)
    copies += [pltpu.make_async_copy(sources[n], held[n], sems.at[cut + n - 2]) for n in range(2, 5)]
    for copy in copies:
        copy.start()
    for n, (low, high) in enumerate(FRAME_CUTS):
        copies[2 * n].wait()
        copies[2 * n + 1].wait()
        for i in range(2):
            for f in range(2):
                terms = [
                    taps_ref[frame - f] * x_ref[i, frame].astype(jnp.float32)
                    for frame in range(low, high)
                    if 0 <= frame - f < TAPS
                ]
                total = functools.reduce(jnp.add, terms)
                total_ref[i * 2 + f] = total if n == 0 else total_ref[i * 2 + f] + total
    for copy in copies[cut:]:
        copy.wait()
    turned = []
    for i in range(2):
        for f in range(2):
            total = total_ref[i * 2 + f]
            y = jnp.dot(
                first_ref[...], total, precision=lax.Precision.HIGHEST, preferred_element_type=jnp.float32
            )
            re, im = y[:64], y[64:]
            cos, sin = turn_ref[0], turn_ref[1]
            turned.append(jnp.concatenate([re * cos + im * sin, im * cos - re * sin], axis=1))
    z = jnp.concatenate(turned, axis=0)
    o = lax.dot_general(
        second_ref[...], z, (((1,), (1,)), ((), ())),
        precision=lax.Precision.HIGHEST, preferred_element_type=jnp.float32,
    )
    for p in range(2):
        for i in range(2):
            for f in range(2):
                at = (i * 2 + f) * 64
                even = o[p * 32 : p * 32 + 32, at : at + 64]
                odd = o[64 + p * 32 : 64 + p * 32 + 32, at : at + 64]
                s = jnp.concatenate([even, odd], axis=1)
                row = (p * 2 + f) * 2 + i
                for k in range(32):
                    lane = (k % 8) * 128
                    rows_ref[k // 8, row : row + 1, lane : lane + 128] = s[k : k + 1]
    for d in range(4):
        outs[d][...] = rows_ref[lax.bitwise_xor(chan_ref[0], d)].astype(jnp.bfloat16)


def spectra(samples, chan):
    x = samples.reshape(2, 17, 2, 64, 128).transpose(0, 1, 3, 2, 4).reshape(2, 17, 128, 128)
    first, turn, second = transform_tables()
    return pl.pallas_call(
        spectra_kernel,
        out_shape=[jax.ShapeDtypeStruct((8, CH_WIN), jnp.bfloat16)] * 4,
        in_specs=[pl.BlockSpec(memory_space=HBM)] * 5 + [pl.BlockSpec(memory_space=SMEM)],
        out_specs=[pl.BlockSpec(memory_space=VMEM)] * 4,
        scratch_shapes=[
            pltpu.VMEM((2, 17, 128, 128), jnp.bfloat16),
            pltpu.VMEM((TAPS, 128, 128), jnp.float32),
            pltpu.VMEM((128, 128), jnp.float32),
            pltpu.VMEM((2, 64, 128), jnp.float32),
            pltpu.VMEM((128, 256), jnp.float32),
            pltpu.SemaphoreType.DMA((2 * len(FRAME_CUTS) + 3,)),
            pltpu.VMEM((4, 128, 128), jnp.float32),
            pltpu.VMEM((4, 8, CH_WIN), jnp.float32),
        ],
        compiler_params=pltpu.CompilerParams(vmem_limit_bytes=56 * MIB),
        name="spectra",
    )(x, jnp.asarray(filter_taps()), jnp.asarray(first), jnp.asarray(turn), jnp.asarray(second), chan)


def group_kernel(chan_ref, *refs):
    pieces, out_ref, wide_ref, rows_ref = refs[:4], refs[4], refs[5], refs[6]
    for d in range(4):
        wide_ref[d] = pieces[d][...].astype(jnp.float32)
    for source in range(4):
        piece = wide_ref[lax.bitwise_xor(chan_ref[0], source)]
        for t in range(4):
            rows_ref[t, source * 2 : source * 2 + 2, :] = piece[t * 2 : t * 2 + 2]
    out_ref[...] = rows_ref[...].reshape(32, CH_WIN).astype(jnp.bfloat16)


def group_spectra(pieces, chan):
    return pl.pallas_call(
        group_kernel,
        out_shape=jax.ShapeDtypeStruct((32, CH_WIN), jnp.bfloat16),
        in_specs=[pl.BlockSpec(memory_space=SMEM)] + [pl.BlockSpec(memory_space=VMEM)] * 4,
        out_specs=pl.BlockSpec(memory_space=VMEM),
        scratch_shapes=[pltpu.VMEM((4, 8, CH_WIN), jnp.float32)] * 2,
        compiler_params=pltpu.CompilerParams(vmem_limit_bytes=8 * MIB),
        name="group_spectra",
    )(chan, *pieces)


def tiles_kernel(base, counts, aliased, *refs):
    slots_ref, own_ref = refs[:2]
    blocks = refs[2 : 2 + len(counts)]
    out_ref, wide_ref, tile_ref, sems = refs[2 + len(counts) + (1 if aliased else 0) :]
    own = own_ref[...].astype(jnp.float32) * 0.5
    for t in range(4):
        for i in range(8):
            wide_ref[i, t] = jnp.broadcast_to(own[t * 8 + i : t * 8 + i + 1], (8, CH_WIN))

    def copy_of(n):
        return pltpu.make_async_copy(tile_ref.at[n], out_ref.at[:, :, slots_ref[0, base + n]], sems.at[n])

    first = 0
    for block_ref, count in zip(blocks, counts, strict=True):

        @pl.loop(0, count)
        def _(index, block_ref=block_ref, first=first):
            n = first + index
            keep = slots_ref[1, base + n].astype(jnp.float32)

            @pl.loop(0, CH_WIN // 128, unroll=UNROLL)
            def _(step):
                lanes = pl.ds(pl.multiple_of(step * 128, 128), 128)
                other = block_ref[index, :, lanes].astype(jnp.float32) * keep
                r0, r1, i0, i1 = (other[t * 8 : t * 8 + 8] for t in range(4))
                for i in range(8):
                    a0, a1, b0, b1 = (wide_ref[i, t, :, lanes] for t in range(4))
                    tile_ref[n, i, 0, :, lanes] = ((a0 * r0 + a1 * r1) + (b0 * i0 + b1 * i1)).astype(jnp.bfloat16)
                    tile_ref[n, i, 1, :, lanes] = ((b0 * r0 + b1 * r1) - (a0 * i0 + a1 * i1)).astype(jnp.bfloat16)

            copy_of(n).start()

        first += count

    @pl.loop(0, first)
    def _(n):
        copy_of(n).wait()


def tiles(slots, base, own, blocks, result, n_slots):
    counts = [block.shape[0] for block in blocks]
    n = sum(counts)
    aliased = result is not None
    operands = [slots, own, *blocks] + ([result] if aliased else [])
    specs = [pl.BlockSpec(memory_space=SMEM)] + [pl.BlockSpec(memory_space=VMEM)] * (1 + len(blocks))
    specs += [pl.BlockSpec(memory_space=pl.ANY)] if aliased else []
    return pl.pallas_call(
        functools.partial(tiles_kernel, base, counts, aliased),
        out_shape=jax.ShapeDtypeStruct((8, 2, n_slots, 8, CH_WIN), jnp.bfloat16),
        in_specs=specs,
        out_specs=pl.BlockSpec(memory_space=pl.ANY),
        input_output_aliases={len(operands) - 1: 0} if aliased else {},
        scratch_shapes=[
            pltpu.VMEM((8, 4, 8, CH_WIN), jnp.float32),
            pltpu.VMEM((n, 8, 2, 8, CH_WIN), jnp.bfloat16),
            pltpu.SemaphoreType.DMA((n,)),
        ],
        compiler_params=pltpu.CompilerParams(vmem_limit_bytes=16 * MIB),
        cost_estimate=pl.CostEstimate(flops=n * 10**5, bytes_accessed=n, transcendentals=0),
        name="tiles",
    )(*operands)


def move(array, target):
    places = [(z, y, x) for z in range(N_Z) for y in range(N_Y) for x in range(N_X)]

    def number(z, y, x):
        return (z % N_Z * N_Y + y % N_Y) * N_X + x % N_X

    return lax.ppermute(array, "stn", [(number(*p), number(*target(*p))) for p in places])


def along_z(array, step):
    return move(array, lambda z, y, x: (z + step, y, x))


def across_y(array):
    return move(array, lambda z, y, x: (z, 1 - y, x))


def swap_x(array, mask):
    return move(array, lambda z, y, x: (z, y, x ^ mask))


def per_device(samples, keeper):
    group = lax.axis_index("stn")
    chan = lax.axis_index("chan")
    z, y, x = group // (N_Y * N_X), group // N_X % N_Y, group % N_X
    n_slots = 33

    chan_scalar = chan.astype(jnp.int32).reshape(1)
    pieces = [
        part if d == 0 else lax.ppermute(part, "chan", [(c, c ^ d) for c in range(4)])
        for d, part in enumerate(spectra(samples, chan_scalar))
    ]
    pieces[0] = jnp.where(chan < 4, pieces[0], jnp.zeros((), jnp.bfloat16))
    own = group_spectra(pieces, chan_scalar)

    z3, z2, z1 = (along_z(own, step) for step in (3, 2, 1))
    z4 = along_z(along_z(own, -2), -2)
    za = jnp.stack([z1, z2])

    def where_from(back, other, mask):
        ry = 1 - y if other else y
        rx = x ^ mask
        if back is None:
            back = jnp.where(ry * N_X + rx < y * N_X + x, 0, 4)
        return ((z - back) % N_Z) * (N_Y * N_X) + ry * N_X + rx

    def froms_a(other):
        return [(back, other, mask) for mask in (0, 1, 3, 2) for back in (1, 2)]

    froms = [
        [(0, 0, 0)] + froms_a(0) + [(3, 0, 0), (4, 0, 0), (3, 1, 0), (None, 1, 0)],
        [(3, 1, 1), (None, 1, 1), (3, 0, 1), (None, 0, 1), (3, 0, 3), (None, 0, 3), (3, 1, 3), (None, 1, 3)],
        froms_a(1) + [(3, 0, 2), (None, 0, 2), (3, 1, 2), (None, 1, 2)],
    ]
    origin = jnp.stack([where_from(*o) for some in froms for o in some]).astype(jnp.int32)
    keep_row = lax.dynamic_index_in_dim(keeper, group, 0, keepdims=False)
    columns = jnp.arange(keeper.shape[1], dtype=jnp.int32)[None, :]
    rank = jnp.sum(jnp.where(columns < origin[:, None], keep_row[None, :], 0), axis=1)
    kept = jnp.sum(jnp.where(columns == origin[:, None], keep_row[None, :], 0), axis=1)
    slots = jnp.stack([jnp.where(kept == 1, rank, n_slots - 1), kept]).astype(jnp.int32)

    bases = [sum(map(len, froms[:n])) for n in range(len(froms))]

    def add(call, blocks, result):
        return tiles(slots, bases[call], own, blocks, result, n_slots)

    a1, a3 = swap_x(za, 1), swap_x(za, 3)
    ar1, ar3 = swap_x(a3[:1], 1), swap_x(a1[1:], 3)
    z3, z4, a1, a3 = lax.optimization_barrier((z3, z4, a1, a3))
    s1, s3, sy = (jnp.where(here, own, z4) for here in (x % 2 == 0, x < 2, y == 0))
    yb = across_y(jnp.stack([z3, sy]))
    row = jnp.concatenate([za, a1, a3, ar1, ar3])
    ya = across_y(row)
    b1 = swap_x(jnp.concatenate([yb, jnp.stack([z3, s1])]), 1)
    b3 = swap_x(jnp.concatenate([jnp.stack([z3, s3]), yb]), 3)
    result = add(0, [own[None], row, z3[None], z4[None], yb], None)
    b1, b3, result = lax.optimization_barrier((b1, b3, result))
    br1, br3 = swap_x(b3[:2], 1), swap_x(b1[:2], 3)
    result = add(1, [b1, b3], result)
    result = add(2, [ya, br1, br3], result)
    return result.reshape(8, 2, n_slots * 8, CH_WIN).swapaxes(2, 3)


def solution(mesh):
    return jax.shard_map(
        per_device,
        mesh=mesh,
        in_specs=(P(("stn", "chan"), None, None, None), P()),
        out_specs=P("stn", None, "chan", None),
        check_vma=False,
    )
```

```python
import functools
import math

import jax
import jax.numpy as jnp
import numpy as np
from jax import lax
from jax.experimental import pallas as pl
from jax.experimental.pallas import tpu as pltpu
from jax.sharding import PartitionSpec as P

NFFT = 8192
TAPS = 16
CH_WIN = 1024
N_Z, N_Y, N_X = 8, 2, 4
MIB = 1 << 20
UNROLL = 8
FRAME_CUTS = ((0, 5), (5, 9), (9, 13), (13, 17))
SMEM = pltpu.MemorySpace.SMEM
VMEM = pltpu.MemorySpace.VMEM
HBM = pltpu.MemorySpace.HBM


def filter_taps():
    pos = np.arange(TAPS * NFFT, dtype=np.float64)
    shifted = (pos + 0.5) / NFFT - TAPS / 2.0
    window = 0.5 - 0.5 * np.cos(2.0 * math.pi * (pos + 0.5) / (TAPS * NFFT))
    taps = (np.sinc(shifted) * window).reshape(TAPS, 64, 1, 128)
    return np.broadcast_to(taps, (TAPS, 64, 2, 128)).reshape(TAPS, 128, 128).astype(np.float32)


def transform_tables():
    k1 = np.arange(64)
    angle = 2.0 * math.pi * (np.outer(k1, k1) % 64) / 64
    cos, sin = np.cos(angle), np.sin(angle)
    first = np.zeros((2, 64, 64, 2))
    first[0, :, :, 0], first[0, :, :, 1] = cos, sin
    first[1, :, :, 0], first[1, :, :, 1] = -sin, cos
    n2 = np.arange(128)
    turn = 2.0 * math.pi * np.outer(k1, n2) / NFFT
    k2 = np.arange(64)
    angle = 2.0 * math.pi * (np.outer(k2, n2) % 128) / 128
    cos = (np.cos(angle) / math.sqrt(NFFT)).reshape(32, 2, 128).transpose(1, 0, 2)
    sin = (np.sin(angle) / math.sqrt(NFFT)).reshape(32, 2, 128).transpose(1, 0, 2)
    second = np.zeros((2, 2, 32, 2, 128))
    second[:, 0, :, 0], second[:, 0, :, 1] = cos, sin
    second[:, 1, :, 0], second[:, 1, :, 1] = -sin, cos
    return (
        first.reshape(128, 128).astype(np.float32),
        np.stack([np.cos(turn), np.sin(turn)]).astype(np.float32),
        second.reshape(128, 256).astype(np.float32),
    )


def spectra_kernel(*refs):
    sources, chan_ref, outs, held, sems, total_ref, rows_ref = refs[:5], refs[5], refs[6:10], refs[10:15], *refs[15:]
    x_ref, taps_ref, first_ref, turn_ref, second_ref = held
    copies = []
    for n, (low, high) in enumerate(FRAME_CUTS):
        frames, taps = pl.ds(low, high - low), pl.ds(low, min(high, TAPS) - low)
        copies.append(pltpu.make_async_copy(sources[0].at[:, frames], x_ref.at[:, frames], sems.at[2 * n]))
        copies.append(pltpu.make_async_copy(sources[1].at[taps], taps_ref.at[taps], sems.at[2 * n + 1]))
    cut = len(copies)
    copies += [pltpu.make_async_copy(sources[n], held[n], sems.at[cut + n - 2]) for n in range(2, 5)]
    for copy in copies:
        copy.start()
    for n, (low, high) in enumerate(FRAME_CUTS):
        copies[2 * n].wait()
        copies[2 * n + 1].wait()
        for i in range(2):
            for f in range(2):
                terms = [
                    taps_ref[frame - f] * x_ref[i, frame].astype(jnp.float32)
                    for frame in range(low, high)
                    if 0 <= frame - f < TAPS
                ]
                total = functools.reduce(jnp.add, terms)
                total_ref[i * 2 + f] = total if n == 0 else total_ref[i * 2 + f] + total
    for copy in copies[cut:]:
        copy.wait()
    turned = []
    for i in range(2):
        for f in range(2):
            total = total_ref[i * 2 + f]
            y = jnp.dot(
                first_ref[...], total, precision=lax.Precision.HIGHEST, preferred_element_type=jnp.float32
            )
            re, im = y[:64], y[64:]
            cos, sin = turn_ref[0], turn_ref[1]
            turned.append(jnp.concatenate([re * cos + im * sin, im * cos - re * sin], axis=1))
    z = jnp.concatenate(turned, axis=0)
    o = lax.dot_general(
        second_ref[...], z, (((1,), (1,)), ((), ())),
        precision=lax.Precision.HIGHEST, preferred_element_type=jnp.float32,
    )
    for p in range(2):
        for i in range(2):
            for f in range(2):
                at = (i * 2 + f) * 64
                even = o[p * 32 : p * 32 + 32, at : at + 64]
                odd = o[64 + p * 32 : 64 + p * 32 + 32, at : at + 64]
                s = jnp.concatenate([even, odd], axis=1)
                row = (p * 2 + f) * 2 + i
                for k in range(32):
                    lane = (k % 8) * 128
                    rows_ref[k // 8, row : row + 1, lane : lane + 128] = s[k : k + 1]
    for d in range(4):
        outs[d][...] = rows_ref[lax.bitwise_xor(chan_ref[0], d)].astype(jnp.bfloat16)


def spectra(samples, chan):
    x = samples.reshape(2, 17, 2, 64, 128).transpose(0, 1, 3, 2, 4).reshape(2, 17, 128, 128)
    first, turn, second = transform_tables()
    return pl.pallas_call(
        spectra_kernel,
        out_shape=[jax.ShapeDtypeStruct((8, CH_WIN), jnp.bfloat16)] * 4,
        in_specs=[pl.BlockSpec(memory_space=HBM)] * 5 + [pl.BlockSpec(memory_space=SMEM)],
        out_specs=[pl.BlockSpec(memory_space=VMEM)] * 4,
        scratch_shapes=[
            pltpu.VMEM((2, 17, 128, 128), jnp.bfloat16),
            pltpu.VMEM((TAPS, 128, 128), jnp.float32),
            pltpu.VMEM((128, 128), jnp.float32),
            pltpu.VMEM((2, 64, 128), jnp.float32),
            pltpu.VMEM((128, 256), jnp.float32),
            pltpu.SemaphoreType.DMA((2 * len(FRAME_CUTS) + 3,)),
            pltpu.VMEM((4, 128, 128), jnp.float32),
            pltpu.VMEM((4, 8, CH_WIN), jnp.float32),
        ],
        compiler_params=pltpu.CompilerParams(vmem_limit_bytes=56 * MIB),
        name="spectra",
    )(x, jnp.asarray(filter_taps()), jnp.asarray(first), jnp.asarray(turn), jnp.asarray(second), chan)


def group_kernel(chan_ref, *refs):
    pieces, out_ref, wide_ref, rows_ref = refs[:4], refs[4], refs[5], refs[6]
    for d in range(4):
        wide_ref[d] = pieces[d][...].astype(jnp.float32)
    for source in range(4):
        piece = wide_ref[lax.bitwise_xor(chan_ref[0], source)]
        for t in range(4):
            rows_ref[t, source * 2 : source * 2 + 2, :] = piece[t * 2 : t * 2 + 2]
    out_ref[...] = rows_ref[...].reshape(32, CH_WIN).astype(jnp.bfloat16)


def group_spectra(pieces, chan):
    return pl.pallas_call(
        group_kernel,
        out_shape=jax.ShapeDtypeStruct((32, CH_WIN), jnp.bfloat16),
        in_specs=[pl.BlockSpec(memory_space=SMEM)] + [pl.BlockSpec(memory_space=VMEM)] * 4,
        out_specs=pl.BlockSpec(memory_space=VMEM),
        scratch_shapes=[pltpu.VMEM((4, 8, CH_WIN), jnp.float32)] * 2,
        compiler_params=pltpu.CompilerParams(vmem_limit_bytes=8 * MIB),
        name="group_spectra",
    )(chan, *pieces)


def tiles_kernel(base, counts, aliased, *refs):
    slots_ref, own_ref = refs[:2]
    blocks = refs[2 : 2 + len(counts)]
    out_ref, wide_ref, tile_ref, sems = refs[2 + len(counts) + (1 if aliased else 0) :]
    own = own_ref[...].astype(jnp.float32) * 0.5
    for t in range(4):
        for pair in range(4):
            at = t * 8 + pair * 2
            two = [jnp.broadcast_to(own[n : n + 1], (8, CH_WIN)) for n in (at, at + 1)]
            wide_ref[pair, t] = jnp.concatenate(two, axis=0).astype(jnp.bfloat16)

    def copy_of(n):
        return pltpu.make_async_copy(tile_ref.at[n], out_ref.at[:, :, slots_ref[0, base + n]], sems.at[n])

    first = 0
    for block_ref, count in zip(blocks, counts, strict=True):

        @pl.loop(0, count)
        def _(index, block_ref=block_ref, first=first):
            n = first + index
            keep = slots_ref[1, base + n].astype(jnp.float32)

            @pl.loop(0, CH_WIN // 128, unroll=UNROLL)
            def _(step):
                lanes = pl.ds(pl.multiple_of(step * 128, 128), 128)
                other = block_ref[index, :, lanes].astype(jnp.float32) * keep
                twice = (other[t * 8 : t * 8 + 8] for t in range(4))
                r0, r1, i0, i1 = (jnp.concatenate([o, o], axis=0).astype(jnp.bfloat16) for o in twice)
                for pair in range(4):
                    a0, a1, b0, b1 = (wide_ref[pair, t, :, lanes] for t in range(4))
                    real = (a0 * r0 + a1 * r1) + (b0 * i0 + b1 * i1)
                    imag = (b0 * r0 + b1 * r1) - (a0 * i0 + a1 * i1)
                    for half in range(2):
                        rows = slice(half * 8, half * 8 + 8)
                        tile_ref[n, pair * 2 + half, 0, :, lanes] = real[rows]
                        tile_ref[n, pair * 2 + half, 1, :, lanes] = imag[rows]

            copy_of(n).start()

        first += count

    @pl.loop(0, first)
    def _(n):
        copy_of(n).wait()


def tiles(slots, base, own, blocks, result, n_slots):
    counts = [block.shape[0] for block in blocks]
    n = sum(counts)
    aliased = result is not None
    operands = [slots, own, *blocks] + ([result] if aliased else [])
    specs = [pl.BlockSpec(memory_space=SMEM)] + [pl.BlockSpec(memory_space=VMEM)] * (1 + len(blocks))
    specs += [pl.BlockSpec(memory_space=pl.ANY)] if aliased else []
    return pl.pallas_call(
        functools.partial(tiles_kernel, base, counts, aliased),
        out_shape=jax.ShapeDtypeStruct((8, 2, n_slots, 8, CH_WIN), jnp.bfloat16),
        in_specs=specs,
        out_specs=pl.BlockSpec(memory_space=pl.ANY),
        input_output_aliases={len(operands) - 1: 0} if aliased else {},
        scratch_shapes=[
            pltpu.VMEM((4, 4, 16, CH_WIN), jnp.bfloat16),
            pltpu.VMEM((n, 8, 2, 8, CH_WIN), jnp.bfloat16),
            pltpu.SemaphoreType.DMA((n,)),
        ],
        compiler_params=pltpu.CompilerParams(vmem_limit_bytes=16 * MIB),
        cost_estimate=pl.CostEstimate(flops=n * 10**5, bytes_accessed=n, transcendentals=0),
        name="tiles",
    )(*operands)


def move(array, target):
    places = [(z, y, x) for z in range(N_Z) for y in range(N_Y) for x in range(N_X)]

    def number(z, y, x):
        return (z % N_Z * N_Y + y % N_Y) * N_X + x % N_X

    return lax.ppermute(array, "stn", [(number(*p), number(*target(*p))) for p in places])


def along_z(array, step):
    return move(array, lambda z, y, x: (z + step, y, x))


def across_y(array):
    return move(array, lambda z, y, x: (z, 1 - y, x))


def swap_x(array, mask):
    return move(array, lambda z, y, x: (z, y, x ^ mask))


def per_device(samples, keeper):
    group = lax.axis_index("stn")
    chan = lax.axis_index("chan")
    z, y, x = group // (N_Y * N_X), group // N_X % N_Y, group % N_X
    n_slots = 33

    chan_scalar = chan.astype(jnp.int32).reshape(1)
    pieces = [
        part if d == 0 else lax.ppermute(part, "chan", [(c, c ^ d) for c in range(4)])
        for d, part in enumerate(spectra(samples, chan_scalar))
    ]
    pieces[0] = jnp.where(chan < 4, pieces[0], jnp.zeros((), jnp.bfloat16))
    own = group_spectra(pieces, chan_scalar)

    z3, z2, z1 = (along_z(own, step) for step in (3, 2, 1))
    z4 = along_z(along_z(own, -2), -2)
    za = jnp.stack([z1, z2])

    def where_from(back, other, mask):
        ry = 1 - y if other else y
        rx = x ^ mask
        if back is None:
            back = jnp.where(ry * N_X + rx < y * N_X + x, 0, 4)
        return ((z - back) % N_Z) * (N_Y * N_X) + ry * N_X + rx

    def froms_a(other):
        return [(back, other, mask) for mask in (0, 1, 3, 2) for back in (1, 2)]

    froms = [
        [(0, 0, 0)] + froms_a(0) + [(3, 0, 0), (4, 0, 0), (3, 1, 0), (None, 1, 0)],
        [(3, 1, 1), (None, 1, 1), (3, 0, 1), (None, 0, 1), (3, 0, 3), (None, 0, 3), (3, 1, 3), (None, 1, 3)],
        froms_a(1) + [(3, 0, 2), (None, 0, 2), (3, 1, 2), (None, 1, 2)],
    ]
    origin = jnp.stack([where_from(*o) for some in froms for o in some]).astype(jnp.int32)
    keep_row = lax.dynamic_index_in_dim(keeper, group, 0, keepdims=False)
    columns = jnp.arange(keeper.shape[1], dtype=jnp.int32)[None, :]
    rank = jnp.sum(jnp.where(columns < origin[:, None], keep_row[None, :], 0), axis=1)
    kept = jnp.sum(jnp.where(columns == origin[:, None], keep_row[None, :], 0), axis=1)
    slots = jnp.stack([jnp.where(kept == 1, rank, n_slots - 1), kept]).astype(jnp.int32)

    bases = [sum(map(len, froms[:n])) for n in range(len(froms))]

    def add(call, blocks, result):
        return tiles(slots, bases[call], own, blocks, result, n_slots)

    a1, a3 = swap_x(za, 1), swap_x(za, 3)
    ar1, ar3 = swap_x(a3[:1], 1), swap_x(a1[1:], 3)
    z3, z4, a1, a3 = lax.optimization_barrier((z3, z4, a1, a3))
    s1, s3, sy = (jnp.where(here, own, z4) for here in (x % 2 == 0, x < 2, y == 0))
    yb = across_y(jnp.stack([z3, sy]))
    row = jnp.concatenate([za, a1, a3, ar1, ar3])
    ya = across_y(row)
    b1 = swap_x(jnp.concatenate([yb, jnp.stack([z3, s1])]), 1)
    b3 = swap_x(jnp.concatenate([jnp.stack([z3, s3]), yb]), 3)
    result = add(0, [own[None], row, z3[None], z4[None], yb], None)
    b1, b3, result = lax.optimization_barrier((b1, b3, result))
    br1, br3 = swap_x(b3[:2], 1), swap_x(b1[:2], 3)
    result = add(1, [b1, b3], result)
    result = add(2, [ya, br1, br3], result)
    return result.reshape(8, 2, n_slots * 8, CH_WIN).swapaxes(2, 3)


def solution(mesh):
    return jax.shard_map(
        per_device,
        mesh=mesh,
        in_specs=(P(("stn", "chan"), None, None, None), P()),
        out_specs=P("stn", None, "chan", None),
        check_vma=False,
    )
```
